32 devices in a mesh: tx: 4 (over z), ty: 8 (over y, x, core).
Axes of the slice: x: 2, y: 2, z: 4, core: 2. Of those that a mesh axis runs over, the one named last changes fastest.
Arguments:
- voxels: bfloat16 [131072, 128], P(('tx', 'ty')), may hold values from 0 to 9
- owner_tile: int32 [131072, 1], P(('tx', 'ty')), may hold values from 0 to 31; in each aligned block of 4096 rows (0 to 4095, 4096 to 8191, ...) at most 256 rows name the same one
- rim_blocks: int32 [32, 4, 16], P(('tx', 'ty')), may hold values from 0 to 127
- kernel_map: int32 [32, 27, 8192], P(('tx', 'ty')), may hold values from -1 to 12287, as said below
- weights: bfloat16 [27, 128, 128], replicated, may hold values from -0.109375 to 0.109375
- norm_gain: float32 [128], replicated, may hold values from 0.1 to 1.9
- shift_bias: float32 [128], replicated, may hold values from -3 to 3
Outputs:
- normalized: bfloat16 [262144, 128], P(('tx', 'ty'))
The draws below stay inside these ranges and needn't reach their ends.
Inputs may be any that keep to these rules, and one draw needn't show every extreme that they name: `owner_tile`: at most 256 of one device's 4096 rows name one tile, and in every draw some device's rows name some tile exactly 256 times. `kernel_map`: for each tile, offset and aligned block of 64 output slots, all entries other than -1 lie in one block of the extended rows. The middle offset maps every slot to itself.
All inputs are finite; a program needn't handle non-finite values.
Results may differ from the reference program's by a relative error of at most 0.0004.
Values may be sent and summed in bfloat16 or wider, within the bound.
A program may use at most 64 MiB of HBM per device.

```python
import math
import jax
import jax.numpy as jnp
import numpy as np
from jax import lax

C_IN = 128
C_OUT = 128
OFFSETS = 27
BLOCK = 64
HB = 16
SRC_ROWS = 4096
TILES = 32
GRID_ROWS = 4
GRID_COLS = 8
PAIR_ROWS = 256
TILE_BLOCKS = 128
TILE_ROWS = 8192
EXT_BLOCKS = 192
TOTAL = 131072


def draw_voxels(key, part):
    key = jax.random.fold_in(key, 11)
    subkeys = jax.random.split(key, 3)
    base = jax.random.normal(subkeys[0], (TOTAL, C_IN), jnp.float32)
    feature = jnp.clip(base, 0.0, 6.0)
    offset = jax.random.uniform(subkeys[2], (1, C_IN), jnp.float32, 0.0, 0.5)
    return (feature + offset).astype(jnp.bfloat16)


def draw_kernel_map(key, part):
    key = jax.random.fold_in(key, 7)
    subkeys = jax.random.split(key, 4)
    block_shape = (TILES, OFFSETS, TILE_BLOCKS)
    slot_shape = (TILES, OFFSETS, TILE_BLOCKS, BLOCK)
    source_block = jax.random.randint(subkeys[0], block_shape, 0, EXT_BLOCKS)
    chance = jax.random.randint(subkeys[1], block_shape, 0, 1000)
    density = 250 + 500 * jnp.arange(TILES, dtype=jnp.int32) // max(TILES - 1, 1)
    present = chance < density[:, None, None]
    within = jax.random.randint(subkeys[2], slot_shape, 0, BLOCK)
    missing = jax.random.randint(subkeys[3], slot_shape, 0, 4) == 0
    mapped = source_block[..., None] * BLOCK + within
    mapped = jnp.where(present[..., None] & jnp.logical_not(missing), mapped, -1)
    centre = jnp.arange(TILE_ROWS, dtype=jnp.int32).reshape(1, TILE_BLOCKS, BLOCK)
    mapped = mapped.at[:, OFFSETS // 2].set(jnp.broadcast_to(centre, (TILES, TILE_BLOCKS, BLOCK)))
    return mapped.reshape(TILES, OFFSETS, TILE_ROWS).astype(jnp.int32)


def place_ends(drawn, stream_key, least, high):
    dims = drawn.shape
    place = [jax.random.randint(jax.random.fold_in(stream_key, axis), (), 0, dims[axis]) for axis in range(len(dims))]
    drawn = drawn.at[tuple(place)].set(least)
    longest = dims.index(max(dims))
    place[longest] = (place[longest] + 1) % dims[longest]
    return drawn.at[tuple(place)].set(high)


def shared_out(rng, own, number, rows, amount, top, reach, skew):
    ranking = jax.random.permutation(rng, amount)
    heavy_load, common = shares(amount, rows * top, reach, skew, True), shares(amount, rows * top, reach, skew, False)
    places = jnp.arange(amount)

    def named(lengths, turn):
        used = int((lengths > 0).sum())
        fixed = max(1, used // 4)
        shifted = fixed + (places - fixed + turn * (used - fixed)) % max(1, amount - fixed)
        return jnp.zeros((amount,), jnp.int32).at[ranking[jnp.where(places < fixed, places, shifted)]].set(jnp.asarray(lengths, jnp.int32))

    lengths = jnp.where(number % 4 == 0, named(heavy_load, number // 4), named(common, number - number // 4 - 1))
    mixed = jax.random.permutation(jax.random.fold_in(own, 3), amount)
    giver, receiver = mixed[0:amount // 2 * 2:2], mixed[1:amount // 2 * 2:2]
    room = jnp.minimum(lengths[giver] - 1, reach - lengths[receiver]) // 2
    room = jnp.where((giver == ranking[0]) | (receiver == ranking[0]) | (lengths[receiver] == 0), 0, jnp.maximum(room, 0))
    shifted = jax.random.randint(jax.random.fold_in(own, 4), (amount // 2,), 0, 1 << 20) % (room + 1)
    lengths = lengths.at[giver].add(-shifted).at[receiver].add(shifted)
    members = jnp.searchsorted(jnp.cumsum(lengths), jnp.arange(rows * top), side="right").astype(jnp.int32)
    table = members.reshape(top, rows).T
    table = table[jax.random.permutation(jax.random.fold_in(own, 1), rows)]
    turn = jax.random.randint(jax.random.fold_in(own, 2), (rows, 1), 0, top)
    return jnp.take_along_axis(table, (jnp.arange(top)[None, :] + turn) % top, axis=1)


def shares(amount, total, bound, slope, full):
    portions = [(1 << 20) // math.isqrt(standing ** slope) + 1 for standing in range(1, amount + 1)]
    largest = bound if full else min(bound, max(-(-total // amount), total * portions[0] // sum(portions)))
    least = 1 if total - largest >= amount - 1 else 0
    given, spare = [largest] + [least] * (amount - 1), total - largest - least * (amount - 1)
    while spare > 0:
        free = [i for i in range(1, amount) if given[i] < largest] or [i for i in range(1, amount) if given[i] < bound]
        pool, budget = sum([portions[i] for i in free]), spare
        for i in free:
            addition = min(bound - given[i], max(1, budget * portions[i] // pool), spare)
            given[i] = given[i] + addition
            spare = spare - addition
    return np.array(given)


def noise(stream_key, extent, deviation, bound, held_as=jnp.bfloat16):
    return jnp.clip(deviation * jax.random.normal(stream_key, extent, jnp.float32), -bound, bound).astype(held_as)


def setup_inputs(seed: int = 0) -> dict:
    streams_of = jax.random.split(jax.random.key(seed), 8)
    voxels = draw_voxels(jax.random.fold_in(streams_of[7], 71), 0)
    owner_tile_keys = jax.random.split(jax.random.fold_in(streams_of[1], 1), TOTAL // SRC_ROWS)
    owner_tile_turns = jax.random.permutation(jax.random.fold_in(streams_of[1], 3), TOTAL // SRC_ROWS)
    owner_tile = jax.vmap(lambda own, number: shared_out(jax.random.fold_in(streams_of[1], 2), own, number, SRC_ROWS, TILES, 1, PAIR_ROWS, 1))(owner_tile_keys, owner_tile_turns).reshape((TOTAL, 1))
    rim_blocks = place_ends(jax.random.randint(streams_of[2], (TILES, 4, HB), 0, TILE_BLOCKS), jax.random.fold_in(streams_of[2], 1), 0, TILE_BLOCKS - 1).astype(jnp.int32)
    kernel_map = draw_kernel_map(jax.random.fold_in(streams_of[7], 71), 0)
    weights = noise(streams_of[4], (OFFSETS, C_IN, C_OUT), (OFFSETS * C_IN) ** -0.5, 0.109375)
    norm_gain = jnp.clip(1.0 + 0.18 * jax.random.normal(streams_of[5], (C_OUT,), jnp.float32), 0.1, 1.9)
    shift_bias = noise(streams_of[6], (C_OUT,), 0.5, 3.0, jnp.float32)
    return {"voxels": voxels, "owner_tile": owner_tile, "rim_blocks": rim_blocks, "kernel_map": kernel_map, "weights": weights, "norm_gain": norm_gain, "shift_bias": shift_bias}


def route_one(bundle):
    payload, targets = bundle
    onehot = (targets[:, None] == jnp.arange(TILES, dtype=jnp.int32)[None, :]).astype(jnp.int32)
    placed = lax.optimization_barrier(jnp.sum((jnp.cumsum(onehot, axis=0) - 1) * onehot, axis=1)).astype(jnp.int32)
    address = (targets * PAIR_ROWS + placed).astype(jnp.int32)
    outgoing = jnp.zeros((TILES * PAIR_ROWS, C_IN), payload.dtype).at[address].set(payload)
    filled = lax.optimization_barrier(jnp.sum(onehot, axis=0)).astype(jnp.int32)
    return (outgoing.reshape(TILES, PAIR_ROWS, C_IN), filled)

def reference(voxels, owner_tile, rim_blocks, kernel_map, weights, norm_gain, shift_bias):
    outgoing, filled = lax.map(route_one, (voxels.reshape(TILES, SRC_ROWS, C_IN), owner_tile.reshape(TILES, SRC_ROWS)))
    arrival = jnp.swapaxes(outgoing, 0, 1).reshape(TILES, TILE_ROWS, C_IN)
    occupied = jnp.arange(PAIR_ROWS, dtype=jnp.int32)[None, None, :] < jnp.swapaxes(filled, 0, 1)[:, :, None]
    occupied = occupied.astype(jnp.float32).reshape(TILES, TILE_ROWS)
    blocked = arrival.reshape(TILES, TILE_BLOCKS, BLOCK, C_IN)
    weights_wide = weights.astype(jnp.float32)

    def one_tile(tile_index):
        grid_row = tile_index // GRID_COLS
        grid_col = tile_index % GRID_COLS
        pieces = [arrival[tile_index]]
        sources = ((tile_index - GRID_COLS, 0, grid_row > 0), (tile_index + GRID_COLS, 1, grid_row < GRID_ROWS - 1), (tile_index - 1, 2, grid_col > 0), (tile_index + 1, 3, grid_col < GRID_COLS - 1))
        for neighbour, direction, present in sources:
            clipped = jnp.clip(neighbour, 0, TILES - 1).astype(jnp.int32)
            chosen = blocked[clipped][rim_blocks[clipped, direction]]
            chosen = jnp.where(present, chosen, jnp.zeros_like(chosen))
            pieces.append(chosen.reshape(HB * BLOCK, C_IN))
        pieces.append(jnp.zeros((1, C_IN), arrival.dtype))
        extended = jnp.concatenate(pieces, axis=0).astype(jnp.float32)
        lookup = jnp.where(kernel_map[tile_index] < 0, EXT_BLOCKS * BLOCK, kernel_map[tile_index]).astype(jnp.int32)
        gathered = extended[lookup]
        response = jnp.einsum('krc,kco->ro', gathered, weights_wide, precision=lax.Precision.HIGHEST)
        return response * occupied[tile_index][:, None]
    response = lax.map(one_tile, jnp.arange(TILES, dtype=jnp.int32))
    average = lax.optimization_barrier(jnp.sum(response, axis=(0, 1))) / TOTAL
    centred = (response - average) * occupied[:, :, None]
    variance = lax.optimization_barrier(jnp.sum(centred * centred, axis=(0, 1))) / TOTAL
    scaled = norm_gain * (response - average) / jnp.sqrt(variance + 1e-05) + shift_bias
    normalized = jnp.maximum(scaled, 0.0) * occupied[:, :, None]
    return normalized.reshape(TILES * TILE_ROWS, C_OUT).astype(jnp.bfloat16)
```

```python
import functools
import jax
import jax.numpy as jnp
from jax import lax
from jax.experimental import pallas as pl
from jax.experimental.pallas import tpu as pltpu
from jax.sharding import PartitionSpec as P

BLOCK = 64
GROUP = 8
MESH = pl.DeviceIdType.MESH


def from_behind(value, axis, steps):
    count = lax.axis_size(axis)
    leading, last = (max(0, -steps), min(count, count - steps))
    return lax.ppermute(value, axis, [(source, source + steps) for source in range(leading, last)])


def place_kernel(address_ref, voxels_ref, out_ref, wide, slots):
    rows = voxels_ref.shape[0]
    total = out_ref.shape[0]
    chunk = 256

    def widen(i, carry):
        at = pl.ds(pl.multiple_of(i * chunk, chunk), chunk)
        wide[at, :] = voxels_ref[at, :].astype(jnp.float32)
        return carry

    def clear(i, carry):
        at = pl.ds(pl.multiple_of(i * chunk, chunk), chunk)
        slots[at, :] = jnp.full((chunk, slots.shape[1]), -1.0, jnp.float32)
        return carry

    def put(i, carry):
        base = pl.multiple_of(i * 16, 16)
        for u in range(16):
            slots[pl.ds(address_ref[base + u], 1), :] = wide[pl.ds(base + u, 1), :]
        return carry

    def narrow(i, carry):
        at = pl.ds(pl.multiple_of(i * chunk, chunk), chunk)
        out_ref[at, :] = slots[at, :].astype(jnp.bfloat16)
        return carry

    lax.fori_loop(0, rows // chunk, widen, 0)
    lax.fori_loop(0, total // chunk, clear, 0)
    lax.fori_loop(0, rows // 16, put, 0)
    lax.fori_loop(0, total // chunk, narrow, 0)


def place(address, voxels, tile_rows):
    rows, channels = voxels.shape
    return pl.pallas_call(
        place_kernel,
        out_shape=jax.ShapeDtypeStruct((tile_rows, channels), jnp.bfloat16),
        in_specs=[
            pl.BlockSpec(memory_space=pltpu.SMEM),
            pl.BlockSpec(memory_space=pltpu.VMEM),
        ],
        out_specs=pl.BlockSpec(memory_space=pltpu.VMEM),
        scratch_shapes=[
            pltpu.VMEM((rows, channels), jnp.float32),
            pltpu.VMEM((tile_rows, channels), jnp.float32),
        ],
        compiler_params=pltpu.CompilerParams(vmem_limit_bytes=32 * 1024 * 1024),
    )(address, voxels)


def conv_kernel(
    sources_ref, used_ref, arrival_ref, lx_ref, ux_ref, ly_ref, uy_ref, local_ref, expand_ref,
    weights_ref, resp_ref, stats_ref, ext, chosen, listed
):
    blocks = arrival_ref.shape[0]
    rim = lx_ref.shape[0]
    pairs = expand_ref.shape[1] // 128
    offsets = 2 * pairs
    channels = arrival_ref.shape[2]
    zero16 = jnp.zeros((BLOCK, channels), jnp.bfloat16)

    def clean(i, carry):
        ext[i] = jnp.maximum(arrival_ref[i], zero16)
        resp_ref[i] = jnp.zeros((BLOCK, channels), jnp.float32)
        return carry

    def clean_rim(i, carry):
        for number, ref in enumerate((lx_ref, ux_ref, ly_ref, uy_ref)):
            ext[blocks + number * rim + i] = jnp.maximum(ref[i], zero16)
        return carry

    lax.fori_loop(0, blocks, clean, 0, unroll=4)
    lax.fori_loop(0, rim, clean_rim, 0)

    def note(b, count):
        taken = used_ref[b]
        listed[count] = b
        return count + taken

    count = lax.fori_loop(0, blocks, note, jnp.int32(0))
    for u in range(GROUP):
        listed[count + u] = listed[jnp.maximum(count - 1, 0)]
    lane = lax.broadcasted_iota(jnp.int32, (1, 128), 1)
    wanted = (lane % BLOCK).astype(jnp.float32)

    def window(w, carry):
        ids = [listed[w * GROUP + u] for u in range(GROUP)]
        local = jnp.concatenate([local_ref[b] for b in ids], axis=0)
        for p in range(pairs):
            spread = jnp.dot(
                local, expand_ref[:, p * 128 : (p + 1) * 128], preferred_element_type=jnp.float32
            )
            selector = jnp.where(spread == wanted, 1.0, 0.0).astype(jnp.bfloat16)
            for u in range(GROUP):
                first = ext[sources_ref[ids[u] * offsets + 2 * p]]
                second = ext[sources_ref[ids[u] * offsets + 2 * p + 1]]
                both = jnp.concatenate(
                    (
                        jnp.concatenate((first, zero16), axis=1),
                        jnp.concatenate((zero16, second), axis=1),
                    ),
                    axis=0,
                )
                picked = jnp.dot(
                    selector[u * BLOCK : (u + 1) * BLOCK], both, preferred_element_type=jnp.float32
                )
                chosen[u * BLOCK : (u + 1) * BLOCK, p * 256 : (p + 1) * 256] = picked.astype(
                    jnp.bfloat16
                )
        for u in range(GROUP):
            chosen[u * BLOCK : (u + 1) * BLOCK, pairs * 256 :] = ext[ids[u]]
        result = jnp.dot(chosen[...], weights_ref[...], preferred_element_type=jnp.float32)
        for u in range(GROUP):
            full = arrival_ref[ids[u]].astype(jnp.float32) >= 0.0
            resp_ref[ids[u]] = jnp.where(full, result[u * BLOCK : (u + 1) * BLOCK], 0.0)
        return carry

    lax.fori_loop(0, (count + GROUP - 1) // GROUP, window, 0)

    def add(i, carry):
        total, number = carry
        full = jnp.where(arrival_ref[i].astype(jnp.float32) >= 0.0, 1.0, 0.0)
        return (
            total + jnp.sum(resp_ref[i].reshape(BLOCK // 8, 8, channels), axis=0),
            number + jnp.sum(full.reshape(BLOCK // 8, 8, channels), axis=0),
        )

    nothing = jnp.zeros((8, channels), jnp.float32)
    total, number = lax.fori_loop(0, blocks, add, (nothing, nothing), unroll=4)
    total = jnp.sum(total, axis=0, keepdims=True)
    number = jnp.sum(number, axis=0, keepdims=True)
    mean = total / jnp.maximum(number, 1.0)

    def spread_of(i, squares):
        full = arrival_ref[i].astype(jnp.float32) >= 0.0
        off = jnp.where(full, resp_ref[i] - mean, 0.0)
        return squares + jnp.sum((off * off).reshape(BLOCK // 8, 8, channels), axis=0)

    squares = lax.fori_loop(0, blocks, spread_of, nothing, unroll=4)
    squares = jnp.sum(squares, axis=0, keepdims=True)
    row = lax.broadcasted_iota(jnp.int32, (8, channels), 0)
    stats_ref[...] = jnp.where(
        row == 0, total, jnp.where(row == 1, squares, jnp.where(row == 2, number, mean))
    )


def convolve(sources, used, arrival, rims, local, expand, weights):
    blocks, _, channels = arrival.shape
    pairs = expand.shape[1] // 128
    smem = pl.BlockSpec(memory_space=pltpu.SMEM)
    vmem = pl.BlockSpec(memory_space=pltpu.VMEM)
    ext_blocks = blocks + 4 * rims[0].shape[0]
    return pl.pallas_call(
        conv_kernel,
        out_shape=(
            jax.ShapeDtypeStruct((blocks, BLOCK, channels), jnp.float32),
            jax.ShapeDtypeStruct((8, channels), jnp.float32),
        ),
        in_specs=[smem, smem] + [vmem] * 8,
        out_specs=(vmem, vmem),
        scratch_shapes=[
            pltpu.VMEM((ext_blocks, BLOCK, channels), jnp.bfloat16),
            pltpu.VMEM((GROUP * BLOCK, pairs * 256 + channels), jnp.bfloat16),
            pltpu.SMEM((blocks + GROUP,), jnp.int32),
        ],
        compiler_params=pltpu.CompilerParams(vmem_limit_bytes=48 * 1024 * 1024),
    )(sources, used, arrival, *rims, local, expand, weights)


def stats_kernel(nx, ny, population, mine_ref, out_ref, along, every, send1, recv1, send2, recv2):
    tx = lax.axis_index("tx")
    ty = lax.axis_index("ty")
    barrier = pltpu.get_barrier_semaphore()
    for d in range(1, ny):
        pl.semaphore_signal(
            barrier, inc=1, device_id=(tx, lax.rem(ty + d, ny)), device_id_type=MESH
        )
    for d in range(1, nx):
        pl.semaphore_signal(
            barrier, inc=1, device_id=(lax.rem(tx + d, nx), ty), device_id_type=MESH
        )
    pl.semaphore_wait(barrier, nx + ny - 2)

    def first(d):
        return pltpu.make_async_remote_copy(
            src_ref=mine_ref,
            dst_ref=along.at[d],
            send_sem=send1.at[d],
            recv_sem=recv1.at[d],
            device_id=(tx, lax.rem(ty + d, ny)),
            device_id_type=MESH,
        )

    def second(d):
        return pltpu.make_async_remote_copy(
            src_ref=along,
            dst_ref=every.at[d],
            send_sem=send2.at[d],
            recv_sem=recv2.at[d],
            device_id=(lax.rem(tx + d, nx), ty),
            device_id_type=MESH,
        )

    for d in range(1, ny):
        first(d).start()
    along[0] = mine_ref[...]
    for d in range(1, ny):
        first(d).wait_recv()
    for d in range(1, nx):
        second(d).start()
    every[0] = along[...]
    for d in range(1, nx):
        second(d).wait_recv()
    for d in range(1, ny):
        first(d).wait_send()
    for d in range(1, nx):
        second(d).wait_send()
    gathered = every[...]
    total = jnp.sum(gathered[:, :, 0:1, :], axis=(0, 1))
    average = total / population
    away = gathered[:, :, 3:4, :] - average[None, None]
    squares = jnp.sum(
        gathered[:, :, 1:2, :] + gathered[:, :, 2:3, :] * away * away, axis=(0, 1)
    )
    variance = squares / population
    row = lax.broadcasted_iota(jnp.int32, out_ref.shape, 0)
    out_ref[...] = jnp.where(row == 0, average, variance)


def combine(stats, population):
    nx = lax.axis_size("tx")
    ny = lax.axis_size("ty")
    channels = stats.shape[1]
    return pl.pallas_call(
        functools.partial(stats_kernel, nx, ny, population),
        out_shape=jax.ShapeDtypeStruct((8, channels), jnp.float32),
        in_specs=[pl.BlockSpec(memory_space=pltpu.VMEM)],
        out_specs=pl.BlockSpec(memory_space=pltpu.VMEM),
        scratch_shapes=[
            pltpu.VMEM((ny, 8, channels), jnp.float32),
            pltpu.VMEM((nx, ny, 8, channels), jnp.float32),
            pltpu.SemaphoreType.DMA((ny,)),
            pltpu.SemaphoreType.DMA((ny,)),
            pltpu.SemaphoreType.DMA((nx,)),
            pltpu.SemaphoreType.DMA((nx,)),
        ],
        compiler_params=pltpu.CompilerParams(collective_id=1, has_side_effects=True),
    )(stats)


def addresses(target, devices, pair_rows):
    src_count = target.shape[0]
    member = (target[:, None] == jnp.arange(devices, dtype=jnp.int32)[None, :]).astype(jnp.bfloat16)
    run_len = min(512, src_count)
    run_count = src_count // run_len
    member_runs = member.reshape(run_count, run_len, devices)
    lower_ones = (jnp.arange(run_len)[:, None] >= jnp.arange(run_len)[None, :]).astype(jnp.bfloat16)
    inside = jnp.einsum("ij,bjd->bid", lower_ones, member_runs, preferred_element_type=jnp.float32)
    run_totals = inside[:, -1, :]
    before = jnp.cumsum(run_totals, axis=0) - run_totals
    running = (inside + before[:, None, :]).reshape(src_count, devices)
    member_wide = member.astype(jnp.float32)
    placed = jnp.sum((running - 1.0) * member_wide, axis=1).astype(jnp.int32)
    return target * pair_rows + placed


def shards(voxels, owner_tile, rim_blocks, kernel_map, weights, norm_gain, shift_bias):
    devices = lax.axis_size(("tx", "ty"))
    channels = voxels.shape[1]
    tile_rows = kernel_map.shape[2]
    offsets = kernel_map.shape[1]
    middle = offsets // 2
    out_blocks = tile_rows // BLOCK
    pair_rows = tile_rows // devices
    address = addresses(owner_tile[:, 0], devices, pair_rows)
    outgoing = place(address, voxels, tile_rows)
    arrival = lax.all_to_all(
        outgoing.reshape(devices, pair_rows, channels),
        ("tx", "ty"),
        split_axis=0,
        concat_axis=0,
        tiled=True,
    )

    around = jnp.concatenate((kernel_map[0, :middle], kernel_map[0, middle + 1 :]), axis=0)
    around = around.T.reshape(out_blocks, BLOCK, offsets - 1)
    source_block = jnp.maximum(jnp.max(around, axis=1) // BLOCK, 0)
    local = jnp.where(around >= 0, around - source_block[:, None, :] * BLOCK, -1)
    local = jnp.pad(local, ((0, 0), (0, 0), (0, 32 - (offsets - 1))), constant_values=-1)
    local = local.astype(jnp.bfloat16)
    width = (offsets - 1) * BLOCK
    expand = (
        jnp.arange(32, dtype=jnp.int32)[:, None] == jnp.arange(width, dtype=jnp.int32)[None, :] // BLOCK
    ).astype(jnp.bfloat16)
    ordered = jnp.concatenate(
        (weights[:middle], weights[middle + 1 :], weights[middle : middle + 1]), axis=0
    ).reshape(offsets * channels, -1)

    blocked = arrival.reshape(out_blocks, BLOCK, channels)
    used = (blocked[:, 0, 0] >= 0).astype(jnp.int32)
    picked = blocked[rim_blocks[0]]
    rims = (
        from_behind(picked[0], "tx", 1),
        from_behind(picked[1], "tx", -1),
        from_behind(picked[2], "ty", 1),
        from_behind(picked[3], "ty", -1),
    )
    response, stats = convolve(
        source_block.reshape(-1), used, blocked, rims, local, expand, ordered
    )
    population = float(voxels.shape[0] * devices)
    combined = combine(stats, population)
    average, variance = combined[0], combined[1]
    response = response.reshape(tile_rows, channels)
    occupied = (arrival.reshape(tile_rows, channels) >= 0).astype(jnp.float32)
    scaled = norm_gain * (response - average) / jnp.sqrt(variance + 1e-05) + shift_bias
    return (jnp.maximum(scaled, 0.0) * occupied).astype(jnp.bfloat16)


def solution(mesh):
    return jax.shard_map(
        shards,
        mesh=mesh,
        in_specs=(
            P(("tx", "ty"), None),
            P(("tx", "ty"), None),
            P(("tx", "ty"), None, None),
            P(("tx", "ty"), None, None),
            P(),
            P(),
            P(),
        ),
        out_specs=P(("tx", "ty"), None),
        check_vma=False,
    )
```

```python
import functools
import jax
import jax.numpy as jnp
from jax import lax
from jax.experimental import pallas as pl
from jax.experimental.pallas import tpu as pltpu
from jax.sharding import PartitionSpec as P

BLOCK = 64
GROUP = 8
MESH = pl.DeviceIdType.MESH


def place_kernel(address_ref, voxels_ref, out_ref, wide, slots):
    rows = voxels_ref.shape[0]
    total = out_ref.shape[0]
    chunk = 256

    def widen(i, carry):
        at = pl.ds(pl.multiple_of(i * chunk, chunk), chunk)
        wide[at, :] = voxels_ref[at, :].astype(jnp.float32)
        return carry

    def clear(i, carry):
        at = pl.ds(pl.multiple_of(i * chunk, chunk), chunk)
        slots[at, :] = jnp.full((chunk, slots.shape[1]), -1.0, jnp.float32)
        return carry

    def put(i, carry):
        base = pl.multiple_of(i * 16, 16)
        for u in range(16):
            slots[pl.ds(address_ref[base + u], 1), :] = wide[pl.ds(base + u, 1), :]
        return carry

    def narrow(i, carry):
        at = pl.ds(pl.multiple_of(i * chunk, chunk), chunk)
        out_ref[at, :] = slots[at, :].astype(jnp.bfloat16)
        return carry

    lax.fori_loop(0, rows // chunk, widen, 0)
    lax.fori_loop(0, total // chunk, clear, 0)
    lax.fori_loop(0, rows // 16, put, 0)
    lax.fori_loop(0, total // chunk, narrow, 0)


def place(address, voxels, tile_rows):
    rows, channels = voxels.shape
    return pl.pallas_call(
        place_kernel,
        out_shape=jax.ShapeDtypeStruct((tile_rows, channels), jnp.bfloat16),
        in_specs=[
            pl.BlockSpec(memory_space=pltpu.SMEM),
            pl.BlockSpec(memory_space=pltpu.VMEM),
        ],
        out_specs=pl.BlockSpec(memory_space=pltpu.VMEM),
        scratch_shapes=[
            pltpu.VMEM((rows, channels), jnp.float32),
            pltpu.VMEM((tile_rows, channels), jnp.float32),
        ],
        compiler_params=pltpu.CompilerParams(vmem_limit_bytes=32 * 1024 * 1024),
    )(address, voxels)


def conv_kernel(
    sources_ref, used_ref, arrival_ref, rims_ref, local_ref, expand_ref, weights_ref,
    resp_ref, stats_ref, ext, chosen, listed
):
    blocks = arrival_ref.shape[0]
    rim = rims_ref.shape[0]
    pairs = expand_ref.shape[1] // 128
    middle = pairs
    channels = arrival_ref.shape[2]
    zero16 = jnp.zeros((BLOCK, channels), jnp.bfloat16)

    def clean(i, carry):
        ext[i] = jnp.maximum(arrival_ref[i], zero16)
        resp_ref[i] = jnp.zeros((BLOCK, channels), jnp.float32)
        return carry

    def clean_rim(i, carry):
        ext[blocks + i] = jnp.maximum(rims_ref[i], zero16)
        return carry

    lax.fori_loop(0, blocks, clean, 0, unroll=4)
    lax.fori_loop(0, rim, clean_rim, 0, unroll=4)

    def note(b, count):
        taken = used_ref[b]
        listed[count] = b
        return count + taken

    count = lax.fori_loop(0, blocks, note, jnp.int32(0))
    for u in range(GROUP):
        listed[count + u] = listed[jnp.maximum(count - 1, 0)]
    lane = lax.broadcasted_iota(jnp.int32, (1, 128), 1)
    wanted = (lane % BLOCK).astype(jnp.float32)

    def window(w, carry):
        ids = [listed[w * GROUP + u] for u in range(GROUP)]
        local = jnp.concatenate([local_ref[b] for b in ids], axis=0)
        for p in range(pairs):
            if p % 2 == 0:
                width = min(256, (pairs - p) * 128)
                spread = jnp.dot(
                    local,
                    expand_ref[:, p * 128 : p * 128 + width],
                    preferred_element_type=jnp.float32,
                )
            here = spread[:, p % 2 * 128 : p % 2 * 128 + 128]
            selector = jnp.where(here == wanted, 1.0, 0.0).astype(jnp.bfloat16)
            k1, k2 = [k + (k >= middle) for k in (2 * p, 2 * p + 1)]
            for u in range(GROUP):
                first = ext[sources_ref[ids[u], k1]]
                second = ext[sources_ref[ids[u], k2]]
                both = jnp.concatenate(
                    (
                        jnp.concatenate((first, zero16), axis=1),
                        jnp.concatenate((zero16, second), axis=1),
                    ),
                    axis=0,
                )
                picked = jnp.dot(
                    selector[u * BLOCK : (u + 1) * BLOCK], both, preferred_element_type=jnp.float32
                )
                chosen[u * BLOCK : (u + 1) * BLOCK, p * 256 : (p + 1) * 256] = picked.astype(
                    jnp.bfloat16
                )
        for u in range(GROUP):
            chosen[u * BLOCK : (u + 1) * BLOCK, pairs * 256 :] = ext[ids[u]]
        result = jnp.dot(chosen[...], weights_ref[...], preferred_element_type=jnp.float32)
        for u in range(GROUP):
            full = arrival_ref[ids[u]].astype(jnp.float32) >= 0.0
            resp_ref[ids[u]] = jnp.where(full, result[u * BLOCK : (u + 1) * BLOCK], 0.0)
        return carry

    lax.fori_loop(0, (count + GROUP - 1) // GROUP, window, 0)

    def add(i, carry):
        total, number = carry
        full = jnp.where(arrival_ref[i].astype(jnp.float32) >= 0.0, 1.0, 0.0)
        return (
            total + jnp.sum(resp_ref[i].reshape(BLOCK // 8, 8, channels), axis=0),
            number + jnp.sum(full.reshape(BLOCK // 8, 8, channels), axis=0),
        )

    nothing = jnp.zeros((8, channels), jnp.float32)
    total, number = lax.fori_loop(0, blocks, add, (nothing, nothing), unroll=4)
    total = jnp.sum(total, axis=0, keepdims=True)
    number = jnp.sum(number, axis=0, keepdims=True)
    mean = total / jnp.maximum(number, 1.0)

    def spread_of(i, squares):
        full = arrival_ref[i].astype(jnp.float32) >= 0.0
        off = jnp.where(full, resp_ref[i] - mean, 0.0)
        return squares + jnp.sum((off * off).reshape(BLOCK // 8, 8, channels), axis=0)

    squares = lax.fori_loop(0, blocks, spread_of, nothing, unroll=4)
    squares = jnp.sum(squares, axis=0, keepdims=True)
    row = lax.broadcasted_iota(jnp.int32, (8, channels), 0)
    stats_ref[...] = jnp.where(
        row == 0, total, jnp.where(row == 1, squares, jnp.where(row == 2, number, mean))
    )


def convolve(sources, used, arrival, rims, local, expand, weights):
    blocks, _, channels = arrival.shape
    pairs = expand.shape[1] // 128
    smem = pl.BlockSpec(memory_space=pltpu.SMEM)
    vmem = pl.BlockSpec(memory_space=pltpu.VMEM)
    ext_blocks = blocks + rims.shape[0]
    return pl.pallas_call(
        conv_kernel,
        out_shape=(
            jax.ShapeDtypeStruct((blocks, BLOCK, channels), jnp.float32),
            jax.ShapeDtypeStruct((8, channels), jnp.float32),
        ),
        in_specs=[smem, smem] + [vmem] * 5,
        out_specs=(vmem, vmem),
        scratch_shapes=[
            pltpu.VMEM((ext_blocks, BLOCK, channels), jnp.bfloat16),
            pltpu.VMEM((GROUP * BLOCK, pairs * 256 + channels), jnp.bfloat16),
            pltpu.SMEM((blocks + GROUP,), jnp.int32),
        ],
        compiler_params=pltpu.CompilerParams(vmem_limit_bytes=48 * 1024 * 1024),
    )(sources, used, arrival, rims, local, expand, weights)


def partner(nx, ny, s):
    tx = lax.rem(lax.axis_index("tx") + lax.rem(s, nx), nx)
    ty = lax.rem(lax.axis_index("ty") + s // nx, ny)
    return tx, ty


def greet(nx, ny):
    barrier = pltpu.get_barrier_semaphore()

    def call(s, carry):
        pl.semaphore_signal(barrier, inc=1, device_id=partner(nx, ny, s), device_id_type=MESH)
        return carry

    lax.fori_loop(1, nx * ny, call, 0)
    pl.semaphore_wait(barrier, nx * ny - 1)


def stats_kernel(nx, ny, population, mine_ref, out_ref, every, send, recv):
    greet(nx, ny)

    def copy(s):
        return pltpu.make_async_remote_copy(
            src_ref=mine_ref,
            dst_ref=every.at[s],
            send_sem=send.at[s],
            recv_sem=recv.at[s],
            device_id=partner(nx, ny, s),
            device_id_type=MESH,
        )

    def start(s, carry):
        copy(s).start()
        return carry

    def finish(s, carry):
        copy(s).wait_recv()
        return carry

    def sent(s, carry):
        copy(s).wait_send()
        return carry

    lax.fori_loop(1, nx * ny, start, 0)
    every[0] = mine_ref[...]
    lax.fori_loop(1, nx * ny, finish, 0)
    lax.fori_loop(1, nx * ny, sent, 0)
    gathered = every[...]
    total = jnp.sum(gathered[:, 0:1, :], axis=0)
    average = total / population
    away = gathered[:, 3:4, :] - average[None]
    squares = jnp.sum(gathered[:, 1:2, :] + gathered[:, 2:3, :] * away * away, axis=0)
    variance = squares / population
    row = lax.broadcasted_iota(jnp.int32, out_ref.shape, 0)
    out_ref[...] = jnp.where(row == 0, average, variance)


def combine(stats, population):
    nx = lax.axis_size("tx")
    ny = lax.axis_size("ty")
    channels = stats.shape[1]
    return pl.pallas_call(
        functools.partial(stats_kernel, nx, ny, population),
        out_shape=jax.ShapeDtypeStruct((8, channels), jnp.float32),
        in_specs=[pl.BlockSpec(memory_space=pltpu.VMEM)],
        out_specs=pl.BlockSpec(memory_space=pltpu.VMEM),
        scratch_shapes=[
            pltpu.VMEM((nx * ny, 8, channels), jnp.float32),
            pltpu.SemaphoreType.DMA((nx * ny,)),
            pltpu.SemaphoreType.DMA((nx * ny,)),
        ],
        compiler_params=pltpu.CompilerParams(collective_id=1, has_side_effects=True),
    )(stats)


def exchange_kernel(
    nx, ny, rim_ref, outgoing_ref, map_ref, arrival_ref, rims_ref, local_ref, sources_ref,
    staged, send, recv, rim_send, rim_recv
):
    tx = lax.axis_index("tx")
    ty = lax.axis_index("ty")
    me = tx * ny + ty
    blocks = arrival_ref.shape[0]
    per = blocks // (nx * ny)
    rim = rims_ref.shape[0] // 4
    greet(nx, ny)

    def copy(s):
        px, py = partner(nx, ny, s)
        return pltpu.make_async_remote_copy(
            src_ref=outgoing_ref.at[pl.ds((px * ny + py) * per, per)],
            dst_ref=arrival_ref.at[pl.ds(me * per, per)],
            send_sem=send.at[s],
            recv_sem=recv.at[s],
            device_id=(px, py),
            device_id_type=MESH,
        )

    def start(s, carry):
        copy(s).start()
        return carry

    def finish(s, carry):
        copy(s).wait_recv()
        return carry

    def sent(s, carry):
        copy(s).wait_send()
        return carry

    lax.fori_loop(1, nx * ny, start, 0)
    for q in range(per):
        arrival_ref[me * per + q] = outgoing_ref[me * per + q]

    def prepare(c, carry):
        turned = map_ref[:, pl.ds(pl.multiple_of(c * 128, 128), 128)].T
        for h in range(2):
            rows = turned[h * BLOCK : (h + 1) * BLOCK]
            source = jnp.maximum(jnp.max(rows, axis=0, keepdims=True), 0) // BLOCK
            local = jnp.where(rows >= 0, rows - source * BLOCK, -1)
            local_ref[2 * c + h] = local.astype(jnp.float32).astype(jnp.bfloat16)
            sources_ref[pl.ds(2 * c + h, 1), :] = source
        return carry

    lax.fori_loop(0, blocks // 2, prepare, 0)
    lax.fori_loop(1, nx * ny, finish, 0)

    def stage(i, carry):
        staged[i] = arrival_ref[rim_ref[i]]
        return carry

    lax.fori_loop(0, 4 * rim, stage, 0)
    ways = (
        (0, (tx + 1, ty), tx < nx - 1, tx > 0),
        (1, (tx - 1, ty), tx > 0, tx < nx - 1),
        (2, (tx, ty + 1), ty < ny - 1, ty > 0),
        (3, (tx, ty - 1), ty > 0, ty < ny - 1),
    )

    def rim_copy(number, to):
        return pltpu.make_async_remote_copy(
            src_ref=staged.at[pl.ds(number * rim, rim)],
            dst_ref=rims_ref.at[pl.ds(number * rim, rim)],
            send_sem=rim_send.at[number],
            recv_sem=rim_recv.at[number],
            device_id=to,
            device_id_type=MESH,
        )

    for number, to, sends, takes in ways:

        @pl.when(sends)
        def _():
            rim_copy(number, to).start()

    for number, to, sends, takes in ways:

        @pl.when(jnp.logical_not(takes))
        def _():
            rims_ref[pl.ds(number * rim, rim)] = jnp.zeros(
                (rim,) + rims_ref.shape[1:], jnp.bfloat16
            )

    for number, to, sends, takes in ways:

        @pl.when(takes)
        def _():
            rim_copy(number, to).wait_recv()

        @pl.when(sends)
        def _():
            rim_copy(number, to).wait_send()

    lax.fori_loop(1, nx * ny, sent, 0)


def exchange(rim_blocks, outgoing, kernel_map):
    nx = lax.axis_size("tx")
    ny = lax.axis_size("ty")
    blocks, _, channels = outgoing.shape
    rims = rim_blocks.shape[0]
    wide = kernel_map.shape[0]
    smem = pl.BlockSpec(memory_space=pltpu.SMEM)
    vmem = pl.BlockSpec(memory_space=pltpu.VMEM)
    return pl.pallas_call(
        functools.partial(exchange_kernel, nx, ny),
        out_shape=(
            jax.ShapeDtypeStruct((blocks, BLOCK, channels), jnp.bfloat16),
            jax.ShapeDtypeStruct((rims, BLOCK, channels), jnp.bfloat16),
            jax.ShapeDtypeStruct((blocks, BLOCK, wide), jnp.bfloat16),
            jax.ShapeDtypeStruct((blocks, wide), jnp.int32),
        ),
        in_specs=[smem, vmem, vmem],
        out_specs=(vmem, vmem, vmem, vmem),
        scratch_shapes=[
            pltpu.VMEM((rims, BLOCK, channels), jnp.bfloat16),
            pltpu.SemaphoreType.DMA((nx * ny,)),
            pltpu.SemaphoreType.DMA((nx * ny,)),
            pltpu.SemaphoreType.DMA((4,)),
            pltpu.SemaphoreType.DMA((4,)),
        ],
        compiler_params=pltpu.CompilerParams(
            collective_id=2, has_side_effects=True, vmem_limit_bytes=48 * 1024 * 1024
        ),
    )(rim_blocks, outgoing, kernel_map)


def addresses(target, devices, pair_rows):
    src_count = target.shape[0]
    member = (target[:, None] == jnp.arange(devices, dtype=jnp.int32)[None, :]).astype(jnp.bfloat16)
    run_len = min(512, src_count)
    run_count = src_count // run_len
    member_runs = member.reshape(run_count, run_len, devices)
    lower_ones = (jnp.arange(run_len)[:, None] >= jnp.arange(run_len)[None, :]).astype(jnp.bfloat16)
    inside = jnp.einsum("ij,bjd->bid", lower_ones, member_runs, preferred_element_type=jnp.float32)
    run_totals = inside[:, -1, :]
    before = jnp.cumsum(run_totals, axis=0) - run_totals
    running = (inside + before[:, None, :]).reshape(src_count, devices)
    member_wide = member.astype(jnp.float32)
    placed = jnp.sum((running - 1.0) * member_wide, axis=1).astype(jnp.int32)
    return target * pair_rows + placed


def shards(voxels, owner_tile, rim_blocks, kernel_map, weights, norm_gain, shift_bias):
    devices = lax.axis_size(("tx", "ty"))
    channels = voxels.shape[1]
    tile_rows = kernel_map.shape[2]
    offsets = kernel_map.shape[1]
    middle = offsets // 2
    out_blocks = tile_rows // BLOCK
    pair_rows = tile_rows // devices
    address = addresses(owner_tile[:, 0], devices, pair_rows)
    outgoing = place(address, voxels, tile_rows)
    padded = jnp.pad(kernel_map[0], ((0, 32 - offsets), (0, 0)), constant_values=-1)
    arrival, rims, local, sources = exchange(
        rim_blocks.reshape(-1), outgoing.reshape(out_blocks, BLOCK, channels), padded
    )
    column = jnp.arange((offsets - 1) * BLOCK, dtype=jnp.int32) // BLOCK
    column = column + (column >= middle)
    expand = (jnp.arange(32, dtype=jnp.int32)[:, None] == column[None, :]).astype(jnp.bfloat16)
    ordered = jnp.concatenate(
        (weights[:middle], weights[middle + 1 :], weights[middle : middle + 1]), axis=0
    ).reshape(offsets * channels, -1)
    used = (arrival[:, 0, 0] >= 0).astype(jnp.int32)
    response, stats = convolve(sources, used, arrival, rims, local, expand, ordered)
    population = float(voxels.shape[0] * devices)
    combined = combine(stats, population)
    average, variance = combined[0], combined[1]
    response = response.reshape(tile_rows, channels)
    occupied = (arrival.reshape(tile_rows, channels) >= 0).astype(jnp.float32)
    scaled = norm_gain * (response - average) / jnp.sqrt(variance + 1e-05) + shift_bias
    return (jnp.maximum(scaled, 0.0) * occupied).astype(jnp.bfloat16)


def solution(mesh):
    return jax.shard_map(
        shards,
        mesh=mesh,
        in_specs=(
            P(("tx", "ty"), None),
            P(("tx", "ty"), None),
            P(("tx", "ty"), None, None),
            P(("tx", "ty"), None, None),
            P(),
            P(),
            P(),
        ),
        out_specs=P(("tx", "ty"), None),
        check_vma=False,
    )
```

```python
import functools
import jax
import jax.numpy as jnp
from jax import lax
from jax.experimental import pallas as pl
from jax.experimental.pallas import tpu as pltpu
from jax.sharding import PartitionSpec as P

BLOCK = 64
MESH = pl.DeviceIdType.MESH


def place_kernel(address_ref, voxels_ref, out_ref, wide, slots):
    rows = voxels_ref.shape[0]
    total = out_ref.shape[0]
    chunk = 256

    def widen(i, carry):
        at = pl.ds(pl.multiple_of(i * chunk, chunk), chunk)
        wide[at, :] = voxels_ref[at, :].astype(jnp.float32)
        return carry

    def clear(i, carry):
        at = pl.ds(pl.multiple_of(i * chunk, chunk), chunk)
        slots[at, :] = jnp.full((chunk, slots.shape[1]), -1.0, jnp.float32)
        return carry

    def put(i, carry):
        base = pl.multiple_of(i * 16, 16)
        for u in range(16):
            slots[pl.ds(address_ref[base + u], 1), :] = wide[pl.ds(base + u, 1), :]
        return carry

    def narrow(i, carry):
        at = pl.ds(pl.multiple_of(i * chunk, chunk), chunk)
        out_ref[at, :] = slots[at, :].astype(jnp.bfloat16)
        return carry

    lax.fori_loop(0, rows // chunk, widen, 0)
    lax.fori_loop(0, total // chunk, clear, 0)
    lax.fori_loop(0, rows // 16, put, 0)
    lax.fori_loop(0, total // chunk, narrow, 0)


def place(address, voxels, tile_rows):
    rows, channels = voxels.shape
    return pl.pallas_call(
        place_kernel,
        out_shape=jax.ShapeDtypeStruct((tile_rows, channels), jnp.bfloat16),
        in_specs=[
            pl.BlockSpec(memory_space=pltpu.SMEM),
            pl.BlockSpec(memory_space=pltpu.VMEM),
        ],
        out_specs=pl.BlockSpec(memory_space=pltpu.VMEM),
        scratch_shapes=[
            pltpu.VMEM((rows, channels), jnp.float32),
            pltpu.VMEM((tile_rows, channels), jnp.float32),
        ],
        compiler_params=pltpu.CompilerParams(vmem_limit_bytes=32 * 1024 * 1024),
    )(address, voxels)


def conv_kernel(
    sources_ref, arrival_ref, rims_ref, map_ref, weights_ref, resp_ref, stats_ref, table, turned
):
    blocks = arrival_ref.shape[0]
    rim = rims_ref.shape[0]
    offsets = weights_ref.shape[0]
    channels = arrival_ref.shape[2]
    middle = offsets // 2
    others = [k for k in range(offsets) if k != middle]
    zero16 = jnp.zeros((BLOCK, channels), jnp.bfloat16)
    lane = lax.broadcasted_iota(jnp.int32, (channels, 128), 1)
    left = lane < BLOCK
    diagonal = lax.broadcasted_iota(jnp.int32, (channels, channels), 0) == (
        lax.broadcasted_iota(jnp.int32, (channels, channels), 1)
    )
    unit = jnp.where(diagonal, 1.0, 0.0).astype(jnp.bfloat16)

    def flip(value):
        return lax.dot_general(
            unit, value, (((1,), (1,)), ((), ())), preferred_element_type=jnp.float32
        )

    def fill(ref, start):
        def step(i, carry):
            one = jnp.maximum(ref[2 * i], zero16)
            two = jnp.maximum(ref[2 * i + 1], zero16)
            both = flip(jnp.concatenate((one, one, two, two), axis=0))
            table[start + 2 * i] = both[:, :128]
            table[start + 2 * i + 1] = both[:, 128:]
            return carry

        lax.fori_loop(0, ref.shape[0] // 2, step, 0, unroll=4)

    fill(arrival_ref, 0)
    fill(rims_ref, blocks)
    for place, k in enumerate(others + [middle]):
        turned[:, place * channels : (place + 1) * channels] = flip(weights_ref[k]).astype(
            jnp.bfloat16
        )

    def window(w, carry):
        def pick(k, c):
            b = 2 * (2 * w + c)
            at = pl.ds(pl.multiple_of((2 * w + c) * 128, 128), 128)
            entry = map_ref[k : k + 1, at]
            spot = lax.rem(jnp.maximum(entry, 0), BLOCK) + jnp.where(left[:1], 0, BLOCK)
            spot = jnp.broadcast_to(spot, (channels, 128))
            source = jnp.where(left, table[sources_ref[b, k]], table[sources_ref[b + 1, k]])
            found = jnp.take_along_axis(source, spot, axis=1)
            return jnp.where(entry >= 0, found, 0.0).astype(jnp.bfloat16)

        def straight(c):
            b = 2 * (2 * w + c)
            return jnp.where(left, table[b], table[b + 1]).astype(jnp.bfloat16)

        result = jnp.dot(
            turned[:, (offsets - 1) * channels :],
            jnp.concatenate((straight(0), straight(1)), axis=1),
            preferred_element_type=jnp.float32,
        )
        for p in range(len(others) // 2):
            k1, k2 = others[2 * p : 2 * p + 2]
            chosen = jnp.concatenate(
                (
                    jnp.concatenate((pick(k1, 0), pick(k1, 1)), axis=1),
                    jnp.concatenate((pick(k2, 0), pick(k2, 1)), axis=1),
                ),
                axis=0,
            )
            result += jnp.dot(
                turned[:, 2 * p * channels : (2 * p + 2) * channels],
                chosen,
                preferred_element_type=jnp.float32,
            )
        for c in range(2):
            rows = result[:, c * 128 : (c + 1) * 128].T
            for h in range(2):
                b = 4 * w + 2 * c + h
                full = arrival_ref[b].astype(jnp.float32) >= 0.0
                resp_ref[b] = jnp.where(full, rows[h * BLOCK : (h + 1) * BLOCK], 0.0)
        return carry

    lax.fori_loop(0, blocks // 4, window, 0)

    def add(i, carry):
        total, number = carry
        full = jnp.where(arrival_ref[i].astype(jnp.float32) >= 0.0, 1.0, 0.0)
        return (
            total + jnp.sum(resp_ref[i].reshape(BLOCK // 8, 8, channels), axis=0),
            number + jnp.sum(full.reshape(BLOCK // 8, 8, channels), axis=0),
        )

    nothing = jnp.zeros((8, channels), jnp.float32)
    total, number = lax.fori_loop(0, blocks, add, (nothing, nothing), unroll=4)
    total = jnp.sum(total, axis=0, keepdims=True)
    number = jnp.sum(number, axis=0, keepdims=True)
    mean = total / jnp.maximum(number, 1.0)

    def spread_of(i, squares):
        full = arrival_ref[i].astype(jnp.float32) >= 0.0
        off = jnp.where(full, resp_ref[i] - mean, 0.0)
        return squares + jnp.sum((off * off).reshape(BLOCK // 8, 8, channels), axis=0)

    squares = lax.fori_loop(0, blocks, spread_of, nothing, unroll=4)
    squares = jnp.sum(squares, axis=0, keepdims=True)
    row = lax.broadcasted_iota(jnp.int32, (8, channels), 0)
    stats_ref[...] = jnp.where(
        row == 0, total, jnp.where(row == 1, squares, jnp.where(row == 2, number, mean))
    )


def convolve(sources, arrival, rims, kernel_map, weights):
    blocks, _, channels = arrival.shape
    offsets = weights.shape[0]
    smem = pl.BlockSpec(memory_space=pltpu.SMEM)
    vmem = pl.BlockSpec(memory_space=pltpu.VMEM)
    ext_blocks = blocks + rims.shape[0]
    return pl.pallas_call(
        conv_kernel,
        out_shape=(
            jax.ShapeDtypeStruct((blocks, BLOCK, channels), jnp.float32),
            jax.ShapeDtypeStruct((8, channels), jnp.float32),
        ),
        in_specs=[smem] + [vmem] * 4,
        out_specs=(vmem, vmem),
        scratch_shapes=[
            pltpu.VMEM((ext_blocks, channels, 128), jnp.float32),
            pltpu.VMEM((channels, offsets * channels), jnp.bfloat16),
        ],
        compiler_params=pltpu.CompilerParams(vmem_limit_bytes=48 * 1024 * 1024),
    )(sources, arrival, rims, kernel_map, weights)


def partner(nx, ny, s):
    tx = lax.rem(lax.axis_index("tx") + lax.rem(s, nx), nx)
    ty = lax.rem(lax.axis_index("ty") + s // nx, ny)
    return tx, ty


def greet(nx, ny):
    barrier = pltpu.get_barrier_semaphore()

    def call(s, carry):
        pl.semaphore_signal(barrier, inc=1, device_id=partner(nx, ny, s), device_id_type=MESH)
        return carry

    lax.fori_loop(1, nx * ny, call, 0)
    pl.semaphore_wait(barrier, nx * ny - 1)


def stats_kernel(nx, ny, population, mine_ref, out_ref, every, send, recv):
    greet(nx, ny)

    def copy(s):
        return pltpu.make_async_remote_copy(
            src_ref=mine_ref,
            dst_ref=every.at[s],
            send_sem=send.at[s],
            recv_sem=recv.at[s],
            device_id=partner(nx, ny, s),
            device_id_type=MESH,
        )

    def start(s, carry):
        copy(s).start()
        return carry

    def finish(s, carry):
        copy(s).wait_recv()
        return carry

    def sent(s, carry):
        copy(s).wait_send()
        return carry

    lax.fori_loop(1, nx * ny, start, 0)
    every[0] = mine_ref[...]
    lax.fori_loop(1, nx * ny, finish, 0)
    lax.fori_loop(1, nx * ny, sent, 0)
    gathered = every[...]
    total = jnp.sum(gathered[:, 0:1, :], axis=0)
    average = total / population
    away = gathered[:, 3:4, :] - average[None]
    squares = jnp.sum(gathered[:, 1:2, :] + gathered[:, 2:3, :] * away * away, axis=0)
    variance = squares / population
    row = lax.broadcasted_iota(jnp.int32, out_ref.shape, 0)
    out_ref[...] = jnp.where(row == 0, average, variance)


def combine(stats, population):
    nx = lax.axis_size("tx")
    ny = lax.axis_size("ty")
    channels = stats.shape[1]
    return pl.pallas_call(
        functools.partial(stats_kernel, nx, ny, population),
        out_shape=jax.ShapeDtypeStruct((8, channels), jnp.float32),
        in_specs=[pl.BlockSpec(memory_space=pltpu.VMEM)],
        out_specs=pl.BlockSpec(memory_space=pltpu.VMEM),
        scratch_shapes=[
            pltpu.VMEM((nx * ny, 8, channels), jnp.float32),
            pltpu.SemaphoreType.DMA((nx * ny,)),
            pltpu.SemaphoreType.DMA((nx * ny,)),
        ],
        compiler_params=pltpu.CompilerParams(collective_id=1, has_side_effects=True),
    )(stats)


def exchange_kernel(
    nx, ny, rim_ref, outgoing_ref, map_ref, arrival_ref, rims_ref, sources_ref,
    staged, send, recv, rim_send, rim_recv
):
    tx = lax.axis_index("tx")
    ty = lax.axis_index("ty")
    me = tx * ny + ty
    blocks = arrival_ref.shape[0]
    per = blocks // (nx * ny)
    rim = rims_ref.shape[0] // 4
    greet(nx, ny)

    def copy(s):
        px, py = partner(nx, ny, s)
        return pltpu.make_async_remote_copy(
            src_ref=outgoing_ref.at[pl.ds((px * ny + py) * per, per)],
            dst_ref=arrival_ref.at[pl.ds(me * per, per)],
            send_sem=send.at[s],
            recv_sem=recv.at[s],
            device_id=(px, py),
            device_id_type=MESH,
        )

    def start(s, carry):
        copy(s).start()
        return carry

    def finish(s, carry):
        copy(s).wait_recv()
        return carry

    def sent(s, carry):
        copy(s).wait_send()
        return carry

    lax.fori_loop(1, nx * ny, start, 0)
    for q in range(per):
        arrival_ref[me * per + q] = outgoing_ref[me * per + q]

    def prepare(c, carry):
        turned = map_ref[:, pl.ds(pl.multiple_of(c * 128, 128), 128)].T
        for h in range(2):
            rows = turned[h * BLOCK : (h + 1) * BLOCK]
            source = jnp.maximum(jnp.max(rows, axis=0, keepdims=True), 0) // BLOCK
            sources_ref[pl.ds(2 * c + h, 1), :] = source
        return carry

    lax.fori_loop(0, blocks // 2, prepare, 0)
    lax.fori_loop(1, nx * ny, finish, 0)

    def stage(i, carry):
        staged[i] = arrival_ref[rim_ref[i]]
        return carry

    lax.fori_loop(0, 4 * rim, stage, 0)
    ways = (
        (0, (tx + 1, ty), tx < nx - 1, tx > 0),
        (1, (tx - 1, ty), tx > 0, tx < nx - 1),
        (2, (tx, ty + 1), ty < ny - 1, ty > 0),
        (3, (tx, ty - 1), ty > 0, ty < ny - 1),
    )

    def rim_copy(number, to):
        return pltpu.make_async_remote_copy(
            src_ref=staged.at[pl.ds(number * rim, rim)],
            dst_ref=rims_ref.at[pl.ds(number * rim, rim)],
            send_sem=rim_send.at[number],
            recv_sem=rim_recv.at[number],
            device_id=to,
            device_id_type=MESH,
        )

    for number, to, sends, takes in ways:

        @pl.when(sends)
        def _():
            rim_copy(number, to).start()

    for number, to, sends, takes in ways:

        @pl.when(jnp.logical_not(takes))
        def _():
            rims_ref[pl.ds(number * rim, rim)] = jnp.zeros(
                (rim,) + rims_ref.shape[1:], jnp.bfloat16
            )

    for number, to, sends, takes in ways:

        @pl.when(takes)
        def _():
            rim_copy(number, to).wait_recv()

        @pl.when(sends)
        def _():
            rim_copy(number, to).wait_send()

    lax.fori_loop(1, nx * ny, sent, 0)


def exchange(rim_blocks, outgoing, kernel_map):
    nx = lax.axis_size("tx")
    ny = lax.axis_size("ty")
    blocks, _, channels = outgoing.shape
    rims = rim_blocks.shape[0]
    wide = kernel_map.shape[0]
    smem = pl.BlockSpec(memory_space=pltpu.SMEM)
    vmem = pl.BlockSpec(memory_space=pltpu.VMEM)
    return pl.pallas_call(
        functools.partial(exchange_kernel, nx, ny),
        out_shape=(
            jax.ShapeDtypeStruct((blocks, BLOCK, channels), jnp.bfloat16),
            jax.ShapeDtypeStruct((rims, BLOCK, channels), jnp.bfloat16),
            jax.ShapeDtypeStruct((blocks, wide), jnp.int32),
        ),
        in_specs=[smem, vmem, vmem],
        out_specs=(vmem, vmem, vmem),
        scratch_shapes=[
            pltpu.VMEM((rims, BLOCK, channels), jnp.bfloat16),
            pltpu.SemaphoreType.DMA((nx * ny,)),
            pltpu.SemaphoreType.DMA((nx * ny,)),
            pltpu.SemaphoreType.DMA((4,)),
            pltpu.SemaphoreType.DMA((4,)),
        ],
        compiler_params=pltpu.CompilerParams(
            collective_id=2, has_side_effects=True, vmem_limit_bytes=48 * 1024 * 1024
        ),
    )(rim_blocks, outgoing, kernel_map)


def addresses(target, devices, pair_rows):
    src_count = target.shape[0]
    member = (target[:, None] == jnp.arange(devices, dtype=jnp.int32)[None, :]).astype(jnp.bfloat16)
    run_len = min(512, src_count)
    run_count = src_count // run_len
    member_runs = member.reshape(run_count, run_len, devices)
    lower_ones = (jnp.arange(run_len)[:, None] >= jnp.arange(run_len)[None, :]).astype(jnp.bfloat16)
    inside = jnp.einsum("ij,bjd->bid", lower_ones, member_runs, preferred_element_type=jnp.float32)
    run_totals = inside[:, -1, :]
    before = jnp.cumsum(run_totals, axis=0) - run_totals
    running = (inside + before[:, None, :]).reshape(src_count, devices)
    member_wide = member.astype(jnp.float32)
    placed = jnp.sum((running - 1.0) * member_wide, axis=1).astype(jnp.int32)
    return target * pair_rows + placed


def shards(voxels, owner_tile, rim_blocks, kernel_map, weights, norm_gain, shift_bias):
    devices = lax.axis_size(("tx", "ty"))
    channels = voxels.shape[1]
    tile_rows = kernel_map.shape[2]
    offsets = kernel_map.shape[1]
    out_blocks = tile_rows // BLOCK
    pair_rows = tile_rows // devices
    address = addresses(owner_tile[:, 0], devices, pair_rows)
    outgoing = place(address, voxels, tile_rows)
    padded = jnp.pad(kernel_map[0], ((0, 32 - offsets), (0, 0)), constant_values=-1)
    arrival, rims, sources = exchange(
        rim_blocks.reshape(-1), outgoing.reshape(out_blocks, BLOCK, channels), padded
    )
    response, stats = convolve(sources, arrival, rims, padded, weights)
    population = float(voxels.shape[0] * devices)
    combined = combine(stats, population)
    average, variance = combined[0], combined[1]
    response = response.reshape(tile_rows, channels)
    occupied = (arrival.reshape(tile_rows, channels) >= 0).astype(jnp.float32)
    scaled = norm_gain * (response - average) / jnp.sqrt(variance + 1e-05) + shift_bias
    return (jnp.maximum(scaled, 0.0) * occupied).astype(jnp.bfloat16)


def solution(mesh):
    return jax.shard_map(
        shards,
        mesh=mesh,
        in_specs=(
            P(("tx", "ty"), None),
            P(("tx", "ty"), None),
            P(("tx", "ty"), None, None),
            P(("tx", "ty"), None, None),
            P(),
            P(),
            P(),
        ),
        out_specs=P(("tx", "ty"), None),
        check_vma=False,
    )
```

```python
import functools
import jax
import jax.numpy as jnp
from jax import lax
from jax.experimental import pallas as pl
from jax.experimental.pallas import tpu as pltpu
from jax.sharding import PartitionSpec as P

BLOCK = 64
MESH = pl.DeviceIdType.MESH


def place_kernel(address_ref, voxels_ref, out_ref, wide, slots):
    rows = voxels_ref.shape[0]
    total = slots.shape[0]
    chunk = 256

    def widen(i, carry):
        at = pl.ds(pl.multiple_of(i * chunk, chunk), chunk)
        wide[at, :] = voxels_ref[at, :].astype(jnp.float32)
        return carry

    def clear(i, carry):
        at = pl.ds(pl.multiple_of(i * chunk, chunk), chunk)
        slots[at, :] = jnp.full((chunk, slots.shape[1]), -1.0, jnp.float32)
        return carry

    def put(i, carry):
        base = pl.multiple_of(i * 16, 16)
        for u in range(16):
            slots[pl.ds(address_ref[base + u], 1), :] = wide[pl.ds(base + u, 1), :]
        return carry

    left = lax.broadcasted_iota(jnp.int32, (BLOCK // 2, slots.shape[1]), 1) < slots.shape[1] // 2

    def narrow(b, carry):
        block = slots[pl.ds(pl.multiple_of(b * BLOCK, BLOCK), BLOCK), :]
        upper, lower = block[: BLOCK // 2], block[BLOCK // 2 :]
        half = slots.shape[1] // 2
        out_ref[0, b] = jnp.where(left, upper, pltpu.roll(lower, half, 1)).astype(jnp.bfloat16)
        out_ref[1, b] = jnp.where(left, pltpu.roll(upper, half, 1), lower).astype(jnp.bfloat16)
        return carry

    lax.fori_loop(0, rows // chunk, widen, 0)
    lax.fori_loop(0, total // chunk, clear, 0)
    lax.fori_loop(0, rows // 16, put, 0)
    lax.fori_loop(0, total // BLOCK, narrow, 0, unroll=4)


def place(address, voxels, tile_rows):
    rows, channels = voxels.shape
    return pl.pallas_call(
        place_kernel,
        out_shape=jax.ShapeDtypeStruct(
            (2, tile_rows // BLOCK, BLOCK // 2, channels), jnp.bfloat16
        ),
        in_specs=[
            pl.BlockSpec(memory_space=pltpu.SMEM),
            pl.BlockSpec(memory_space=pltpu.VMEM),
        ],
        out_specs=pl.BlockSpec(memory_space=pltpu.VMEM),
        scratch_shapes=[
            pltpu.VMEM((rows, channels), jnp.float32),
            pltpu.VMEM((tile_rows, channels), jnp.float32),
        ],
        compiler_params=pltpu.CompilerParams(vmem_limit_bytes=32 * 1024 * 1024),
    )(address, voxels)


def partner(nx, ny, s):
    tx = lax.rem(lax.axis_index("tx") + lax.rem(s, nx), nx)
    ty = lax.rem(lax.axis_index("ty") + s // nx, ny)
    return tx, ty


def layer_kernel(
    nx, ny, population, rim_ref, outgoing_ref, map_ref, weights_ref, resp_ref, out_ref,
    arrival0, arrival1, staged, rims, found_v, found_s, table, turned, partial, filled, mine, every,
    send, recv, rim_send, rim_recv, stat_send, stat_recv, local_sem
):
    tx = lax.axis_index("tx")
    ty = lax.axis_index("ty")
    me = tx * ny + ty
    count = nx * ny
    arrival = (arrival0, arrival1)
    blocks = arrival0.shape[0]
    per = blocks // count
    rim = rims.shape[1] // 4
    offsets = weights_ref.shape[0]
    channels = weights_ref.shape[1]
    half = channels // 2
    middle = offsets // 2
    order = [k for k in range(offsets) if k != middle] + [middle]

    barrier = pltpu.get_barrier_semaphore()

    def call(s, carry):
        pl.semaphore_signal(barrier, inc=1, device_id=partner(nx, ny, s), device_id_type=MESH)
        return carry

    lax.fori_loop(1, count, call, 0)
    pl.semaphore_wait(barrier, count - 1)

    def copy(h, s):
        px, py = partner(nx, ny, s)
        return pltpu.make_async_remote_copy(
            src_ref=outgoing_ref.at[h, pl.ds((px * ny + py) * per, per)],
            dst_ref=arrival[h].at[pl.ds(me * per, per)],
            send_sem=send.at[h, s],
            recv_sem=recv.at[h, s],
            device_id=(px, py),
            device_id_type=MESH,
        )

    def each(act):
        def step(s, carry):
            act(s)
            return carry

        lax.fori_loop(1, count, step, 0)

    ways = (
        (0, (tx + 1, ty), tx < nx - 1, tx > 0),
        (1, (tx - 1, ty), tx > 0, tx < nx - 1),
        (2, (tx, ty + 1), ty < ny - 1, ty > 0),
        (3, (tx, ty - 1), ty > 0, ty < ny - 1),
    )

    def rim_copy(h, number, to):
        return pltpu.make_async_remote_copy(
            src_ref=staged.at[h, pl.ds(number * rim, rim)],
            dst_ref=rims.at[h, pl.ds(number * rim, rim)],
            send_sem=rim_send.at[h, number],
            recv_sem=rim_recv.at[h, number],
            device_id=to,
            device_id_type=MESH,
        )

    def send_rims(h):
        def stage(i, carry):
            staged[h, i] = arrival[h][rim_ref[i]]
            return carry

        lax.fori_loop(0, 4 * rim, stage, 0)
        for number, to, sends, takes in ways:

            @pl.when(sends)
            def _():
                rim_copy(h, number, to).start()

            @pl.when(jnp.logical_not(takes))
            def _():
                rims[h, pl.ds(number * rim, rim)] = jnp.zeros((rim,) + rims.shape[2:], jnp.bfloat16)

    def take_rims(h):
        for number, to, sends, takes in ways:

            @pl.when(takes)
            def _():
                rim_copy(h, number, to).wait_recv()

    def drain(h):
        each(lambda s: copy(h, s).wait_send())
        for number, to, sends, takes in ways:

            @pl.when(sends)
            def _():
                rim_copy(h, number, to).wait_send()

    each(lambda s: copy(0, s).start())
    for h in range(2):
        for q in range(per):
            arrival[h][me * per + q] = outgoing_ref[h, me * per + q]

    found_v[...] = jnp.zeros_like(found_v)

    def prepare(c, carry):
        columns = map_ref[:, pl.ds(pl.multiple_of(c * 128, 128), 128)].T
        for i in range(2):
            rows = columns[i * BLOCK : (i + 1) * BLOCK]
            source = jnp.maximum(jnp.max(rows, axis=0, keepdims=True), 0) // BLOCK
            found_v[pl.ds(2 * c + i, 1), 0 : map_ref.shape[0]] = source
        return carry

    lax.fori_loop(0, blocks // 2, prepare, 0)
    inward = pltpu.make_async_copy(found_v, found_s, local_sem)
    inward.start()

    row_at = lax.broadcasted_iota(jnp.int32, (channels, channels), 0)
    lane_at = lax.broadcasted_iota(jnp.int32, (channels, channels), 1)
    unit = jnp.where(row_at == lane_at, 1.0, 0.0).astype(jnp.bfloat16)
    top_at = lax.broadcasted_iota(jnp.int32, (half, 2 * channels), 0)
    wide_at = lax.broadcasted_iota(jnp.int32, (half, 2 * channels), 1)
    halves = (wide_at == top_at) | (wide_at == top_at + channels + half)
    halves = jnp.where(halves, 1.0, 0.0).astype(jnp.bfloat16)
    left = lane_at[:half] < BLOCK

    def flip(value, by):
        return lax.dot_general(
            by, value, (((1,), (1,)), ((), ())), preferred_element_type=jnp.float32
        )

    nothing16 = jnp.zeros((half, channels), jnp.bfloat16)
    for h in range(2):
        for p in range((offsets + 1) // 2):
            one = weights_ref[order[2 * p]][h * half : (h + 1) * half]
            two = nothing16
            if 2 * p + 1 < offsets:
                two = weights_ref[order[2 * p + 1]][h * half : (h + 1) * half]
            turned[h, :, p * channels : (p + 1) * channels] = flip(
                jnp.concatenate((one, two), axis=0), unit
            ).astype(jnp.bfloat16)
    inward.wait()

    quiet = jnp.zeros((BLOCK // 2, channels), jnp.bfloat16)

    def block_table(block):
        first = jnp.concatenate((block, quiet, block, quiet), axis=0)
        second = jnp.concatenate((quiet, block, quiet, block), axis=0)
        return flip(jnp.concatenate((first, second), axis=1), halves)

    def fill_tile(h):
        def step(c, carry):
            one = block_table(arrival[h][2 * c])
            two = block_table(arrival[h][2 * c + 1])
            table[2 * c] = jnp.maximum(one, 0.0)
            table[2 * c + 1] = jnp.maximum(two, 0.0)
            if h == 1:
                filled[c] = jnp.where(left[:8], one[:8], two[:8])
            return carry

        lax.fori_loop(0, blocks // 2, step, 0, unroll=4)

    def fill_rims(h):
        def step(i, carry):
            table[blocks + i] = jnp.maximum(block_table(rims[h, i]), 0.0)
            return carry

        lax.fori_loop(0, 4 * rim, step, 0, unroll=4)

    marker = -1e30

    def convolve(h):
        def window(w, carry):
            def pick(k, c):
                b = 2 * (2 * w + c)
                if k == middle:
                    return jnp.where(left, table[b], table[b + 1]).astype(jnp.bfloat16)
                at = pl.ds(pl.multiple_of((2 * w + c) * 128, 128), 128)
                entry = map_ref[k : k + 1, at]
                spot = lax.rem(jnp.maximum(entry, 0), BLOCK) + jnp.where(left[:1], 0, BLOCK)
                spot = jnp.broadcast_to(spot, (half, 128))
                source = jnp.where(left, table[found_s[b, k]], table[found_s[b + 1, k]])
                taken = jnp.take_along_axis(source, spot, axis=1)
                return jnp.where(entry >= 0, taken, 0.0).astype(jnp.bfloat16)

            result = None
            for p in range((offsets + 3) // 4):
                parts = [
                    jnp.concatenate((pick(k, 0), pick(k, 1)), axis=1)
                    for k in order[4 * p : 4 * p + 4]
                ]
                while len(parts) % 2:
                    parts.append(jnp.zeros((half, 256), jnp.bfloat16))
                depth = len(parts) * half
                term = jnp.dot(
                    turned[h, :, p * 4 * half : p * 4 * half + depth],
                    jnp.concatenate(parts, axis=0),
                    preferred_element_type=jnp.float32,
                )
                result = term if result is None else result + term
            if h == 0:
                partial[w] = result
            else:
                result = result + partial[w]
                for c in range(2):
                    here = filled[2 * w + c][0:1] >= 0.0
                    rows = jnp.where(here, result[:, c * 128 : (c + 1) * 128], marker).T
                    resp_ref[pl.ds(pl.multiple_of((2 * w + c) * 128, 128), 128), :] = rows
            return carry

        lax.fori_loop(0, blocks // 4, window, 0)

    each(lambda s: copy(0, s).wait_recv())
    send_rims(0)
    each(lambda s: copy(1, s).start())
    fill_tile(0)
    take_rims(0)
    fill_rims(0)
    convolve(0)
    each(lambda s: copy(1, s).wait_recv())
    send_rims(1)
    fill_tile(1)
    take_rims(1)
    fill_rims(1)
    convolve(1)

    def rows_of(i):
        value = resp_ref[pl.ds(pl.multiple_of(i * BLOCK, BLOCK), BLOCK), :]
        return value, value > marker * 0.5

    def fold(value):
        return jnp.sum(value.reshape(BLOCK // 8, 8, channels), axis=0)

    def add(i, carry):
        value, full = rows_of(i)
        return (
            carry[0] + fold(jnp.where(full, value, 0.0)),
            carry[1] + fold(jnp.where(full, 1.0, 0.0)),
        )

    nothing = jnp.zeros((8, channels), jnp.float32)
    total, number = lax.fori_loop(0, blocks, add, (nothing, nothing), unroll=4)
    total = jnp.sum(total, axis=0, keepdims=True)
    number = jnp.sum(number, axis=0, keepdims=True)
    mean = total / jnp.maximum(number, 1.0)

    def spread_of(i, squares):
        value, full = rows_of(i)
        off = jnp.where(full, value - mean, 0.0)
        return squares + fold(off * off)

    squares = lax.fori_loop(0, blocks, spread_of, nothing, unroll=4)
    squares = jnp.sum(squares, axis=0, keepdims=True)
    row = lax.broadcasted_iota(jnp.int32, (8, channels), 0)
    stats = jnp.where(
        row == 0, total, jnp.where(row == 1, squares, jnp.where(row == 2, number, mean))
    )
    mine[...] = stats
    every[0] = stats

    def stat_copy(s):
        return pltpu.make_async_remote_copy(
            src_ref=mine,
            dst_ref=every.at[s],
            send_sem=stat_send.at[s],
            recv_sem=stat_recv.at[s],
            device_id=partner(nx, ny, s),
            device_id_type=MESH,
        )

    each(lambda s: stat_copy(s).start())
    drain(0)
    drain(1)
    each(lambda s: stat_copy(s).wait_recv())
    gathered = every[...]
    average = jnp.sum(gathered[:, 0:1, :], axis=0) / population
    away = gathered[:, 3:4, :] - average[None]
    squares = jnp.sum(gathered[:, 1:2, :] + gathered[:, 2:3, :] * away * away, axis=0)
    out_ref[...] = jnp.where(row == 0, average, squares / population)
    each(lambda s: stat_copy(s).wait_send())


def layer(rim_blocks, outgoing, kernel_map, weights, population):
    nx = lax.axis_size("tx")
    ny = lax.axis_size("ty")
    count = nx * ny
    _, blocks, block_half, channels = outgoing.shape
    rims = rim_blocks.shape[0]
    offsets = weights.shape[0]
    smem = pl.BlockSpec(memory_space=pltpu.SMEM)
    vmem = pl.BlockSpec(memory_space=pltpu.VMEM)
    dma = pltpu.SemaphoreType.DMA
    return pl.pallas_call(
        functools.partial(layer_kernel, nx, ny, population),
        out_shape=(
            jax.ShapeDtypeStruct((blocks * BLOCK, channels), jnp.float32),
            jax.ShapeDtypeStruct((8, channels), jnp.float32),
        ),
        in_specs=[smem, vmem, vmem, vmem],
        out_specs=(vmem, vmem),
        scratch_shapes=[
            pltpu.VMEM((blocks, block_half, channels), jnp.bfloat16),
            pltpu.VMEM((blocks, block_half, channels), jnp.bfloat16),
            pltpu.VMEM((2, rims, block_half, channels), jnp.bfloat16),
            pltpu.VMEM((2, rims, block_half, channels), jnp.bfloat16),
            pltpu.VMEM((blocks, 128), jnp.int32),
            pltpu.SMEM((blocks, 128), jnp.int32),
            pltpu.VMEM((blocks + rims, channels // 2, 128), jnp.float32),
            pltpu.VMEM((2, channels, (offsets + 1) // 2 * channels), jnp.bfloat16),
            pltpu.VMEM((blocks // 4, channels, 256), jnp.float32),
            pltpu.VMEM((blocks // 2, 8, 128), jnp.float32),
            pltpu.VMEM((8, channels), jnp.float32),
            pltpu.VMEM((count, 8, channels), jnp.float32),
            dma((2, count)),
            dma((2, count)),
            dma((2, 4)),
            dma((2, 4)),
            dma((count,)),
            dma((count,)),
            dma(()),
        ],
        compiler_params=pltpu.CompilerParams(
            collective_id=1, has_side_effects=True, vmem_limit_bytes=48 * 1024 * 1024
        ),
    )(rim_blocks, outgoing, kernel_map, weights)


def addresses(target, devices, pair_rows):
    src_count = target.shape[0]
    member = (target[:, None] == jnp.arange(devices, dtype=jnp.int32)[None, :]).astype(jnp.bfloat16)
    run_len = min(512, src_count)
    run_count = src_count // run_len
    member_runs = member.reshape(run_count, run_len, devices)
    lower_ones = (jnp.arange(run_len)[:, None] >= jnp.arange(run_len)[None, :]).astype(jnp.bfloat16)
    inside = jnp.einsum("ij,bjd->bid", lower_ones, member_runs, preferred_element_type=jnp.float32)
    run_totals = inside[:, -1, :]
    before = jnp.cumsum(run_totals, axis=0) - run_totals
    running = (inside + before[:, None, :]).reshape(src_count, devices)
    member_wide = member.astype(jnp.float32)
    placed = jnp.sum((running - 1.0) * member_wide, axis=1).astype(jnp.int32)
    return target * pair_rows + placed


def shards(voxels, owner_tile, rim_blocks, kernel_map, weights, norm_gain, shift_bias):
    devices = lax.axis_size(("tx", "ty"))
    channels = voxels.shape[1]
    tile_rows = kernel_map.shape[2]
    offsets = kernel_map.shape[1]
    pair_rows = tile_rows // devices
    address = addresses(owner_tile[:, 0], devices, pair_rows)
    outgoing = place(address, voxels, tile_rows)
    padded = jnp.pad(kernel_map[0], ((0, 32 - offsets), (0, 0)), constant_values=-1)
    population = float(voxels.shape[0] * devices)
    response, combined = layer(rim_blocks.reshape(-1), outgoing, padded, weights, population)
    average, variance = combined[0], combined[1]
    scaled = norm_gain * (response - average) / jnp.sqrt(variance + 1e-05) + shift_bias
    return jnp.where(response > -5e29, jnp.maximum(scaled, 0.0), 0.0).astype(jnp.bfloat16)


def solution(mesh):
    return jax.shard_map(
        shards,
        mesh=mesh,
        in_specs=(
            P(("tx", "ty"), None),
            P(("tx", "ty"), None),
            P(("tx", "ty"), None, None),
            P(("tx", "ty"), None, None),
            P(),
            P(),
            P(),
        ),
        out_specs=P(("tx", "ty"), None),
        check_vma=False,
    )
```

```python
import functools
import jax
import jax.numpy as jnp
from jax import lax
from jax.experimental import pallas as pl
from jax.experimental.pallas import tpu as pltpu
from jax.sharding import PartitionSpec as P

BLOCK = 64
MESH = pl.DeviceIdType.MESH


def place_kernel(address_ref, voxels_ref, out_ref, wide, slots):
    rows = voxels_ref.shape[0]
    total = slots.shape[0]
    chunk = 256

    def widen(i, carry):
        at = pl.ds(pl.multiple_of(i * chunk, chunk), chunk)
        wide[at, :] = voxels_ref[at, :].astype(jnp.float32)
        return carry

    def clear(i, carry):
        at = pl.ds(pl.multiple_of(i * chunk, chunk), chunk)
        slots[at, :] = jnp.full((chunk, slots.shape[1]), -1.0, jnp.float32)
        return carry

    def put(i, carry):
        base = pl.multiple_of(i * 16, 16)
        for u in range(16):
            slots[pl.ds(address_ref[base + u], 1), :] = wide[pl.ds(base + u, 1), :]
        return carry

    left = lax.broadcasted_iota(jnp.int32, (BLOCK // 2, slots.shape[1]), 1) < slots.shape[1] // 2

    def narrow(b, carry):
        block = slots[pl.ds(pl.multiple_of(b * BLOCK, BLOCK), BLOCK), :]
        upper, lower = block[: BLOCK // 2], block[BLOCK // 2 :]
        half = slots.shape[1] // 2
        out_ref[0, b] = jnp.where(left, upper, pltpu.roll(lower, half, 1)).astype(jnp.bfloat16)
        out_ref[1, b] = jnp.where(left, pltpu.roll(upper, half, 1), lower).astype(jnp.bfloat16)
        return carry

    lax.fori_loop(0, rows // chunk, widen, 0)
    lax.fori_loop(0, total // chunk, clear, 0)
    lax.fori_loop(0, rows // 16, put, 0)
    lax.fori_loop(0, total // BLOCK, narrow, 0, unroll=4)


def place(address, voxels, tile_rows):
    rows, channels = voxels.shape
    return pl.pallas_call(
        place_kernel,
        out_shape=jax.ShapeDtypeStruct(
            (2, tile_rows // BLOCK, BLOCK // 2, channels), jnp.bfloat16
        ),
        in_specs=[
            pl.BlockSpec(memory_space=pltpu.SMEM),
            pl.BlockSpec(memory_space=pltpu.VMEM),
        ],
        out_specs=pl.BlockSpec(memory_space=pltpu.VMEM),
        scratch_shapes=[
            pltpu.VMEM((rows, channels), jnp.float32),
            pltpu.VMEM((tile_rows, channels), jnp.float32),
        ],
        compiler_params=pltpu.CompilerParams(vmem_limit_bytes=32 * 1024 * 1024),
    )(address, voxels)


def partner(nx, ny, s):
    tx = lax.rem(lax.axis_index("tx") + lax.rem(s, nx), nx)
    ty = lax.rem(lax.axis_index("ty") + s // nx, ny)
    return tx, ty


def layer_kernel(
    nx, ny, population, rim_ref, outgoing_ref, map_ref, weights_ref, resp_ref, out_ref,
    arrival0, arrival1, staged, rims, found_v, found_s, spots, table, turned, partial, filled, mine, every,
    send, recv, rim_send, rim_recv, stat_send, stat_recv, local_sem
):
    tx = lax.axis_index("tx")
    ty = lax.axis_index("ty")
    me = tx * ny + ty
    count = nx * ny
    arrival = (arrival0, arrival1)
    blocks = arrival0.shape[0]
    per = blocks // count
    rim = rims.shape[1] // 4
    offsets = weights_ref.shape[0]
    channels = weights_ref.shape[1]
    half = channels // 2
    middle = offsets // 2
    order = [k for k in range(offsets) if k != middle] + [middle]

    barrier = pltpu.get_barrier_semaphore()

    def call(s, carry):
        pl.semaphore_signal(barrier, inc=1, device_id=partner(nx, ny, s), device_id_type=MESH)
        return carry

    lax.fori_loop(1, count, call, 0)
    pl.semaphore_wait(barrier, count - 1)

    def copy(h, s):
        px, py = partner(nx, ny, s)
        return pltpu.make_async_remote_copy(
            src_ref=outgoing_ref.at[h, pl.ds((px * ny + py) * per, per)],
            dst_ref=arrival[h].at[pl.ds(me * per, per)],
            send_sem=send.at[h, s],
            recv_sem=recv.at[h, s],
            device_id=(px, py),
            device_id_type=MESH,
        )

    def each(act):
        def step(s, carry):
            act(s)
            return carry

        lax.fori_loop(1, count, step, 0)

    ways = (
        (0, (tx + 1, ty), tx < nx - 1, tx > 0),
        (1, (tx - 1, ty), tx > 0, tx < nx - 1),
        (2, (tx, ty + 1), ty < ny - 1, ty > 0),
        (3, (tx, ty - 1), ty > 0, ty < ny - 1),
    )

    def rim_copy(h, number, to):
        return pltpu.make_async_remote_copy(
            src_ref=staged.at[h, pl.ds(number * rim, rim)],
            dst_ref=rims.at[h, pl.ds(number * rim, rim)],
            send_sem=rim_send.at[h, number],
            recv_sem=rim_recv.at[h, number],
            device_id=to,
            device_id_type=MESH,
        )

    def send_rims(h):
        def stage(i, carry):
            for number in range(4):
                staged[h, number * rim + i] = arrival[h][rim_ref[number, i]]
            return carry

        lax.fori_loop(0, rim, stage, 0)
        for number, to, sends, takes in ways:

            @pl.when(sends)
            def _():
                rim_copy(h, number, to).start()

            @pl.when(jnp.logical_not(takes))
            def _():
                rims[h, pl.ds(number * rim, rim)] = jnp.zeros((rim,) + rims.shape[2:], jnp.bfloat16)

    def take_rims(h):
        for number, to, sends, takes in ways:

            @pl.when(takes)
            def _():
                rim_copy(h, number, to).wait_recv()

    def drain(h):
        each(lambda s: copy(h, s).wait_send())
        for number, to, sends, takes in ways:

            @pl.when(sends)
            def _():
                rim_copy(h, number, to).wait_send()

    each(lambda s: copy(0, s).start())
    for h in range(2):
        for q in range(per):
            arrival[h][me * per + q] = outgoing_ref[h, me * per + q]

    found_v[...] = jnp.zeros_like(found_v)

    second = jnp.where(
        lax.broadcasted_iota(jnp.int32, (map_ref.shape[0], 128), 1) < BLOCK, 0, BLOCK
    )

    def prepare(c, carry):
        at = pl.ds(pl.multiple_of(c * 128, 128), 128)
        entries = map_ref[:, at]
        spots[:, at] = jnp.bitwise_and(entries, BLOCK - 1) + second
        columns = entries.T
        for i in range(2):
            rows = columns[i * BLOCK : (i + 1) * BLOCK]
            source = jnp.maximum(jnp.max(rows, axis=0, keepdims=True), 0) // BLOCK
            found_v[pl.ds(2 * c + i, 1), 0 : map_ref.shape[0]] = source
        return carry

    lax.fori_loop(0, blocks // 2, prepare, 0)
    inward = pltpu.make_async_copy(found_v, found_s, local_sem)
    inward.start()

    row_at = lax.broadcasted_iota(jnp.int32, (channels, channels), 0)
    lane_at = lax.broadcasted_iota(jnp.int32, (channels, channels), 1)
    unit = jnp.where(row_at == lane_at, 1.0, 0.0).astype(jnp.bfloat16)
    top_at = lax.broadcasted_iota(jnp.int32, (half, 2 * channels), 0)
    wide_at = lax.broadcasted_iota(jnp.int32, (half, 2 * channels), 1)
    halves = (wide_at == top_at) | (wide_at == top_at + channels + half)
    halves = jnp.where(halves, 1.0, 0.0).astype(jnp.bfloat16)
    left = lane_at[:half] < BLOCK

    def flip(value, by):
        return lax.dot_general(
            by, value, (((1,), (1,)), ((), ())), preferred_element_type=jnp.float32
        )

    nothing16 = jnp.zeros((half, channels), jnp.bfloat16)
    for h in range(2):
        for p in range((offsets + 1) // 2):
            one = weights_ref[order[2 * p]][h * half : (h + 1) * half]
            two = nothing16
            if 2 * p + 1 < offsets:
                two = weights_ref[order[2 * p + 1]][h * half : (h + 1) * half]
            turned[h, :, p * channels : (p + 1) * channels] = flip(
                jnp.concatenate((one, two), axis=0), unit
            ).astype(jnp.bfloat16)
    inward.wait()

    quiet = jnp.zeros((BLOCK // 2, channels), jnp.bfloat16)

    def block_table(block):
        first = jnp.concatenate((block, quiet, block, quiet), axis=0)
        second = jnp.concatenate((quiet, block, quiet, block), axis=0)
        return flip(jnp.concatenate((first, second), axis=1), halves)

    def fill_tile(h):
        def step(c, carry):
            one = block_table(arrival[h][2 * c])
            two = block_table(arrival[h][2 * c + 1])
            table[2 * c] = jnp.maximum(one, 0.0)
            table[2 * c + 1] = jnp.maximum(two, 0.0)
            if h == 1:
                filled[c] = jnp.where(left[:8], one[:8], two[:8])
            return carry

        lax.fori_loop(0, blocks // 2, step, 0, unroll=4)

    def fill_rims(h):
        def step(i, carry):
            table[blocks + i] = jnp.maximum(block_table(rims[h, i]), 0.0)
            return carry

        lax.fori_loop(0, 4 * rim, step, 0, unroll=4)

    marker = -1e30

    def convolve(h, first, last):
        def window(w, carry):
            def pick(k, c):
                b = 2 * (2 * w + c)
                if k == middle:
                    return jnp.where(left, table[b], table[b + 1]).astype(jnp.bfloat16)
                at = pl.ds(pl.multiple_of((2 * w + c) * 128, 128), 128)
                entry = map_ref[k : k + 1, at]
                spot = jnp.broadcast_to(spots[k : k + 1, at], (half, 128))
                source = jnp.where(left, table[found_s[b, k]], table[found_s[b + 1, k]])
                taken = jnp.take_along_axis(source, spot, axis=1)
                return jnp.where(entry >= 0, taken, 0.0).astype(jnp.bfloat16)

            result = None
            for p in range((offsets + 3) // 4):
                parts = [
                    jnp.concatenate((pick(k, 0), pick(k, 1)), axis=1)
                    for k in order[4 * p : 4 * p + 4]
                ]
                while len(parts) % 2:
                    parts.append(jnp.zeros((half, 256), jnp.bfloat16))
                depth = len(parts) * half
                term = jnp.dot(
                    turned[h, :, p * 4 * half : p * 4 * half + depth],
                    jnp.concatenate(parts, axis=0),
                    preferred_element_type=jnp.float32,
                )
                result = term if result is None else result + term
            if h == 0:
                partial[w] = result
            else:
                result = result + partial[w]
                for c in range(2):
                    here = filled[2 * w + c][0:1] >= 0.0
                    rows = jnp.where(here, result[:, c * 128 : (c + 1) * 128], marker).T
                    resp_ref[pl.ds(pl.multiple_of((2 * w + c) * 128, 128), 128), :] = rows
            return carry

        lax.fori_loop(first, last, window, 0)

    each(lambda s: copy(0, s).wait_recv())
    send_rims(0)
    each(lambda s: copy(1, s).start())
    fill_tile(0)
    take_rims(0)
    fill_rims(0)
    windows = blocks // 4
    split = windows * 3 // 4
    convolve(0, 0, split)
    each(lambda s: copy(1, s).wait_recv())
    send_rims(1)
    convolve(0, split, windows)
    fill_tile(1)
    take_rims(1)
    fill_rims(1)
    convolve(1, 0, windows)

    def rows_of(i):
        value = resp_ref[pl.ds(pl.multiple_of(i * BLOCK, BLOCK), BLOCK), :]
        return value, value > marker * 0.5

    def fold(value):
        return jnp.sum(value.reshape(BLOCK // 8, 8, channels), axis=0)

    def add(i, carry):
        value, full = rows_of(i)
        return (
            carry[0] + fold(jnp.where(full, value, 0.0)),
            carry[1] + fold(jnp.where(full, 1.0, 0.0)),
        )

    nothing = jnp.zeros((8, channels), jnp.float32)
    total, number = lax.fori_loop(0, blocks, add, (nothing, nothing), unroll=4)
    total = jnp.sum(total, axis=0, keepdims=True)
    number = jnp.sum(number, axis=0, keepdims=True)
    mean = total / jnp.maximum(number, 1.0)

    def spread_of(i, squares):
        value, full = rows_of(i)
        off = jnp.where(full, value - mean, 0.0)
        return squares + fold(off * off)

    squares = lax.fori_loop(0, blocks, spread_of, nothing, unroll=4)
    squares = jnp.sum(squares, axis=0, keepdims=True)
    row = lax.broadcasted_iota(jnp.int32, (8, channels), 0)
    stats = jnp.where(
        row == 0, total, jnp.where(row == 1, squares, jnp.where(row == 2, number, mean))
    )
    mine[...] = stats
    every[0] = stats

    def stat_copy(s):
        return pltpu.make_async_remote_copy(
            src_ref=mine,
            dst_ref=every.at[s],
            send_sem=stat_send.at[s],
            recv_sem=stat_recv.at[s],
            device_id=partner(nx, ny, s),
            device_id_type=MESH,
        )

    each(lambda s: stat_copy(s).start())
    drain(0)
    drain(1)
    each(lambda s: stat_copy(s).wait_recv())
    gathered = every[...]
    average = jnp.sum(gathered[:, 0:1, :], axis=0) / population
    away = gathered[:, 3:4, :] - average[None]
    squares = jnp.sum(gathered[:, 1:2, :] + gathered[:, 2:3, :] * away * away, axis=0)
    out_ref[...] = jnp.where(row == 0, average, squares / population)
    each(lambda s: stat_copy(s).wait_send())


def layer(rim_blocks, outgoing, kernel_map, weights, population):
    nx = lax.axis_size("tx")
    ny = lax.axis_size("ty")
    count = nx * ny
    _, blocks, block_half, channels = outgoing.shape
    rims = rim_blocks.shape[0] * rim_blocks.shape[1]
    offsets = weights.shape[0]
    smem = pl.BlockSpec(memory_space=pltpu.SMEM)
    vmem = pl.BlockSpec(memory_space=pltpu.VMEM)
    dma = pltpu.SemaphoreType.DMA
    return pl.pallas_call(
        functools.partial(layer_kernel, nx, ny, population),
        out_shape=(
            jax.ShapeDtypeStruct((blocks * BLOCK, channels), jnp.float32),
            jax.ShapeDtypeStruct((8, channels), jnp.float32),
        ),
        in_specs=[smem, vmem, vmem, vmem],
        out_specs=(vmem, vmem),
        scratch_shapes=[
            pltpu.VMEM((blocks, block_half, channels), jnp.bfloat16),
            pltpu.VMEM((blocks, block_half, channels), jnp.bfloat16),
            pltpu.VMEM((2, rims, block_half, channels), jnp.bfloat16),
            pltpu.VMEM((2, rims, block_half, channels), jnp.bfloat16),
            pltpu.VMEM((blocks, 128), jnp.int32),
            pltpu.SMEM((blocks, 128), jnp.int32),
            pltpu.VMEM(kernel_map.shape, jnp.int32),
            pltpu.VMEM((blocks + rims, channels // 2, 128), jnp.float32),
            pltpu.VMEM((2, channels, (offsets + 1) // 2 * channels), jnp.bfloat16),
            pltpu.VMEM((blocks // 4, channels, 256), jnp.float32),
            pltpu.VMEM((blocks // 2, 8, 128), jnp.float32),
            pltpu.VMEM((8, channels), jnp.float32),
            pltpu.VMEM((count, 8, channels), jnp.float32),
            dma((2, count)),
            dma((2, count)),
            dma((2, 4)),
            dma((2, 4)),
            dma((count,)),
            dma((count,)),
            dma(()),
        ],
        compiler_params=pltpu.CompilerParams(
            collective_id=1, has_side_effects=True, vmem_limit_bytes=48 * 1024 * 1024
        ),
    )(rim_blocks, outgoing, kernel_map, weights)


def addresses(target, devices, pair_rows):
    src_count = target.shape[0]
    member = (target[:, None] == jnp.arange(devices, dtype=jnp.int32)[None, :]).astype(jnp.bfloat16)
    run_len = min(512, src_count)
    run_count = src_count // run_len
    member_runs = member.reshape(run_count, run_len, devices)
    lower_ones = (jnp.arange(run_len)[:, None] >= jnp.arange(run_len)[None, :]).astype(jnp.bfloat16)
    inside = jnp.einsum("ij,bjd->bid", lower_ones, member_runs, preferred_element_type=jnp.float32)
    run_totals = inside[:, -1, :]
    before = jnp.cumsum(run_totals, axis=0) - run_totals
    running = (inside + before[:, None, :]).reshape(src_count, devices)
    member_wide = member.astype(jnp.float32)
    placed = jnp.sum((running - 1.0) * member_wide, axis=1).astype(jnp.int32)
    return target * pair_rows + placed


def shards(voxels, owner_tile, rim_blocks, kernel_map, weights, norm_gain, shift_bias):
    devices = lax.axis_size(("tx", "ty"))
    channels = voxels.shape[1]
    tile_rows = kernel_map.shape[2]
    offsets = kernel_map.shape[1]
    pair_rows = tile_rows // devices
    address = addresses(owner_tile[:, 0], devices, pair_rows)
    outgoing = place(address, voxels, tile_rows)
    padded = jnp.pad(kernel_map[0], ((0, 32 - offsets), (0, 0)), constant_values=-1)
    population = float(voxels.shape[0] * devices)
    response, combined = layer(rim_blocks[0], outgoing, padded, weights, population)
    average, variance = combined[0], combined[1]
    scaled = norm_gain * (response - average) / jnp.sqrt(variance + 1e-05) + shift_bias
    return jnp.where(response > -5e29, jnp.maximum(scaled, 0.0), 0.0).astype(jnp.bfloat16)


def solution(mesh):
    return jax.shard_map(
        shards,
        mesh=mesh,
        in_specs=(
            P(("tx", "ty"), None),
            P(("tx", "ty"), None),
            P(("tx", "ty"), None, None),
            P(("tx", "ty"), None, None),
            P(),
            P(),
            P(),
        ),
        out_specs=P(("tx", "ty"), None),
        check_vma=False,
    )
```

```python
import functools
import jax
import jax.numpy as jnp
from jax import lax
from jax.experimental import pallas as pl
from jax.experimental.pallas import tpu as pltpu
from jax.sharding import PartitionSpec as P

BLOCK = 64
MESH = pl.DeviceIdType.MESH


def place_kernel(address_ref, voxels_ref, out_ref, wide, slots):
    rows = voxels_ref.shape[0]
    total = slots.shape[0]
    chunk = 256

    def widen(i, carry):
        at = pl.ds(pl.multiple_of(i * chunk, chunk), chunk)
        wide[at, :] = voxels_ref[at, :].astype(jnp.float32)
        return carry

    def clear(i, carry):
        at = pl.ds(pl.multiple_of(i * chunk, chunk), chunk)
        slots[at, :] = jnp.full((chunk, slots.shape[1]), -1.0, jnp.float32)
        return carry

    def put(i, carry):
        base = pl.multiple_of(i * 16, 16)
        for u in range(16):
            slots[pl.ds(address_ref[base + u], 1), :] = wide[pl.ds(base + u, 1), :]
        return carry

    left = lax.broadcasted_iota(jnp.int32, (BLOCK // 2, slots.shape[1]), 1) < slots.shape[1] // 2

    def narrow(b, carry):
        block = slots[pl.ds(pl.multiple_of(b * BLOCK, BLOCK), BLOCK), :]
        upper, lower = block[: BLOCK // 2], block[BLOCK // 2 :]
        half = slots.shape[1] // 2
        out_ref[0, b] = jnp.where(left, upper, pltpu.roll(lower, half, 1)).astype(jnp.bfloat16)
        out_ref[1, b] = jnp.where(left, pltpu.roll(upper, half, 1), lower).astype(jnp.bfloat16)
        return carry

    lax.fori_loop(0, rows // chunk, widen, 0)
    lax.fori_loop(0, total // chunk, clear, 0)
    lax.fori_loop(0, rows // 16, put, 0)
    lax.fori_loop(0, total // BLOCK, narrow, 0, unroll=4)


def place(address, voxels, tile_rows):
    rows, channels = voxels.shape
    return pl.pallas_call(
        place_kernel,
        out_shape=jax.ShapeDtypeStruct(
            (2, tile_rows // BLOCK, BLOCK // 2, channels), jnp.bfloat16
        ),
        in_specs=[
            pl.BlockSpec(memory_space=pltpu.SMEM),
            pl.BlockSpec(memory_space=pltpu.VMEM),
        ],
        out_specs=pl.BlockSpec(memory_space=pltpu.VMEM),
        scratch_shapes=[
            pltpu.VMEM((rows, channels), jnp.float32),
            pltpu.VMEM((tile_rows, channels), jnp.float32),
        ],
        compiler_params=pltpu.CompilerParams(vmem_limit_bytes=32 * 1024 * 1024),
    )(address, voxels)


def partner(nx, ny, s):
    tx = lax.rem(lax.axis_index("tx") + lax.rem(s, nx), nx)
    ty = lax.rem(lax.axis_index("ty") + s // nx, ny)
    return tx, ty


def layer_kernel(
    nx, ny, population, rim_ref, outgoing_ref, map_ref, weights_ref, affine_ref, out_ref, resp_ref,
    arrival0, arrival1, staged, rims, found_v, found_s, spots, table, turned, partial, filled, mine, every,
    send, recv, rim_send, rim_recv, stat_send, stat_recv, local_sem
):
    tx = lax.axis_index("tx")
    ty = lax.axis_index("ty")
    me = tx * ny + ty
    count = nx * ny
    arrival = (arrival0, arrival1)
    blocks = arrival0.shape[0]
    per = blocks // count
    rim = rims.shape[1] // 4
    offsets = weights_ref.shape[0]
    channels = weights_ref.shape[1]
    half = channels // 2
    middle = offsets // 2
    order = [k for k in range(offsets) if k != middle] + [middle]

    barrier = pltpu.get_barrier_semaphore()

    def call(s, carry):
        pl.semaphore_signal(barrier, inc=1, device_id=partner(nx, ny, s), device_id_type=MESH)
        return carry

    lax.fori_loop(1, count, call, 0)
    pl.semaphore_wait(barrier, count - 1)

    def copy(h, s):
        px, py = partner(nx, ny, s)
        return pltpu.make_async_remote_copy(
            src_ref=outgoing_ref.at[h, pl.ds((px * ny + py) * per, per)],
            dst_ref=arrival[h].at[pl.ds(me * per, per)],
            send_sem=send.at[h, s],
            recv_sem=recv.at[h, s],
            device_id=(px, py),
            device_id_type=MESH,
        )

    def each(act):
        def step(s, carry):
            act(s)
            return carry

        lax.fori_loop(1, count, step, 0)

    ways = (
        (0, (tx + 1, ty), tx < nx - 1, tx > 0),
        (1, (tx - 1, ty), tx > 0, tx < nx - 1),
        (2, (tx, ty + 1), ty < ny - 1, ty > 0),
        (3, (tx, ty - 1), ty > 0, ty < ny - 1),
    )

    def rim_copy(h, number, to):
        return pltpu.make_async_remote_copy(
            src_ref=staged.at[h, pl.ds(number * rim, rim)],
            dst_ref=rims.at[h, pl.ds(number * rim, rim)],
            send_sem=rim_send.at[h, number],
            recv_sem=rim_recv.at[h, number],
            device_id=to,
            device_id_type=MESH,
        )

    def send_rims(h):
        def stage(i, carry):
            for number in range(4):
                staged[h, number * rim + i] = arrival[h][rim_ref[number, i]]
            return carry

        lax.fori_loop(0, rim, stage, 0)
        for number, to, sends, takes in ways:

            @pl.when(sends)
            def _():
                rim_copy(h, number, to).start()

            @pl.when(jnp.logical_not(takes))
            def _():
                rims[h, pl.ds(number * rim, rim)] = jnp.zeros((rim,) + rims.shape[2:], jnp.bfloat16)

    def take_rims(h):
        for number, to, sends, takes in ways:

            @pl.when(takes)
            def _():
                rim_copy(h, number, to).wait_recv()

    def drain(h):
        each(lambda s: copy(h, s).wait_send())
        for number, to, sends, takes in ways:

            @pl.when(sends)
            def _():
                rim_copy(h, number, to).wait_send()

    each(lambda s: copy(0, s).start())
    for h in range(2):
        for q in range(per):
            arrival[h][me * per + q] = outgoing_ref[h, me * per + q]

    found_v[...] = jnp.zeros_like(found_v)

    second = jnp.where(
        lax.broadcasted_iota(jnp.int32, (map_ref.shape[0], 128), 1) < BLOCK, 0, BLOCK
    )

    def prepare(c, carry):
        at = pl.ds(pl.multiple_of(c * 128, 128), 128)
        entries = map_ref[:, at]
        spots[:, at] = jnp.bitwise_and(entries, BLOCK - 1) + second
        columns = entries.T
        for i in range(2):
            rows = columns[i * BLOCK : (i + 1) * BLOCK]
            source = jnp.maximum(jnp.max(rows, axis=0, keepdims=True), 0) // BLOCK
            found_v[pl.ds(2 * c + i, 1), 0 : map_ref.shape[0]] = source
        return carry

    lax.fori_loop(0, blocks // 2, prepare, 0)
    inward = pltpu.make_async_copy(found_v, found_s, local_sem)
    inward.start()

    row_at = lax.broadcasted_iota(jnp.int32, (channels, channels), 0)
    lane_at = lax.broadcasted_iota(jnp.int32, (channels, channels), 1)
    unit = jnp.where(row_at == lane_at, 1.0, 0.0).astype(jnp.bfloat16)
    top_at = lax.broadcasted_iota(jnp.int32, (half, 2 * channels), 0)
    wide_at = lax.broadcasted_iota(jnp.int32, (half, 2 * channels), 1)
    halves = (wide_at == top_at) | (wide_at == top_at + channels + half)
    halves = jnp.where(halves, 1.0, 0.0).astype(jnp.bfloat16)
    left = lane_at[:half] < BLOCK

    def flip(value, by):
        return lax.dot_general(
            by, value, (((1,), (1,)), ((), ())), preferred_element_type=jnp.float32
        )

    nothing16 = jnp.zeros((half, channels), jnp.bfloat16)
    for h in range(2):
        for p in range((offsets + 1) // 2):
            one = weights_ref[order[2 * p]][h * half : (h + 1) * half]
            two = nothing16
            if 2 * p + 1 < offsets:
                two = weights_ref[order[2 * p + 1]][h * half : (h + 1) * half]
            turned[h, :, p * channels : (p + 1) * channels] = flip(
                jnp.concatenate((one, two), axis=0), unit
            ).astype(jnp.bfloat16)
    inward.wait()

    quiet = jnp.zeros((BLOCK // 2, channels), jnp.bfloat16)

    def block_table(block):
        first = jnp.concatenate((block, quiet, block, quiet), axis=0)
        second = jnp.concatenate((quiet, block, quiet, block), axis=0)
        return flip(jnp.concatenate((first, second), axis=1), halves)

    def fill_tile(h):
        def step(c, carry):
            one = block_table(arrival[h][2 * c])
            two = block_table(arrival[h][2 * c + 1])
            table[2 * c] = jnp.maximum(one, 0.0)
            table[2 * c + 1] = jnp.maximum(two, 0.0)
            if h == 1:
                filled[c] = jnp.where(left[:8], one[:8], two[:8])
            return carry

        lax.fori_loop(0, blocks // 2, step, 0, unroll=4)

    def fill_rims(h):
        def step(i, carry):
            table[blocks + i] = jnp.maximum(block_table(rims[h, i]), 0.0)
            return carry

        lax.fori_loop(0, 4 * rim, step, 0, unroll=4)

    marker = -1e30

    def convolve(h, first, last):
        def window(w, carry):
            def pick(k, c):
                b = 2 * (2 * w + c)
                if k == middle:
                    return jnp.where(left, table[b], table[b + 1]).astype(jnp.bfloat16)
                at = pl.ds(pl.multiple_of((2 * w + c) * 128, 128), 128)
                entry = map_ref[k : k + 1, at]
                spot = jnp.broadcast_to(spots[k : k + 1, at], (half, 128))
                source = jnp.where(left, table[found_s[b, k]], table[found_s[b + 1, k]])
                taken = jnp.take_along_axis(source, spot, axis=1)
                return jnp.where(entry >= 0, taken, 0.0).astype(jnp.bfloat16)

            result = None
            for p in range((offsets + 3) // 4):
                parts = [
                    jnp.concatenate((pick(k, 0), pick(k, 1)), axis=1)
                    for k in order[4 * p : 4 * p + 4]
                ]
                while len(parts) % 2:
                    parts.append(jnp.zeros((half, 256), jnp.bfloat16))
                depth = len(parts) * half
                term = jnp.dot(
                    turned[h, :, p * 4 * half : p * 4 * half + depth],
                    jnp.concatenate(parts, axis=0),
                    preferred_element_type=jnp.float32,
                )
                result = term if result is None else result + term
            if h == 0:
                partial[w] = result
            else:
                result = result + partial[w]
                for c in range(2):
                    here = filled[2 * w + c][0:1] >= 0.0
                    rows = jnp.where(here, result[:, c * 128 : (c + 1) * 128], marker).T
                    resp_ref[pl.ds(pl.multiple_of((2 * w + c) * 128, 128), 128), :] = rows
            return carry

        lax.fori_loop(first, last, window, 0)

    each(lambda s: copy(0, s).wait_recv())
    send_rims(0)
    fill_tile(0)
    take_rims(0)
    each(lambda s: copy(1, s).start())
    fill_rims(0)
    windows = blocks // 4
    split = windows * 7 // 8
    convolve(0, 0, split)
    each(lambda s: copy(1, s).wait_recv())
    send_rims(1)
    convolve(0, split, windows)
    fill_tile(1)
    take_rims(1)
    fill_rims(1)
    convolve(1, 0, windows)

    def rows_of(i):
        value = resp_ref[pl.ds(pl.multiple_of(i * BLOCK, BLOCK), BLOCK), :]
        return value, value > marker * 0.5

    def fold(value):
        return jnp.sum(value.reshape(BLOCK // 8, 8, channels), axis=0)

    def add(i, carry):
        value, full = rows_of(i)
        return (
            carry[0] + fold(jnp.where(full, value, 0.0)),
            carry[1] + fold(jnp.where(full, 1.0, 0.0)),
        )

    nothing = jnp.zeros((8, channels), jnp.float32)
    total, number = lax.fori_loop(0, blocks, add, (nothing, nothing), unroll=4)
    total = jnp.sum(total, axis=0, keepdims=True)
    number = jnp.sum(number, axis=0, keepdims=True)
    mean = total / jnp.maximum(number, 1.0)

    def spread_of(i, squares):
        value, full = rows_of(i)
        off = jnp.where(full, value - mean, 0.0)
        return squares + fold(off * off)

    squares = lax.fori_loop(0, blocks, spread_of, nothing, unroll=4)
    squares = jnp.sum(squares, axis=0, keepdims=True)
    row = lax.broadcasted_iota(jnp.int32, (8, channels), 0)
    stats = jnp.where(
        row == 0, total, jnp.where(row == 1, squares, jnp.where(row == 2, number, mean))
    )
    mine[...] = stats
    every[0] = stats

    def stat_copy(s):
        return pltpu.make_async_remote_copy(
            src_ref=mine,
            dst_ref=every.at[s],
            send_sem=stat_send.at[s],
            recv_sem=stat_recv.at[s],
            device_id=partner(nx, ny, s),
            device_id_type=MESH,
        )

    each(lambda s: stat_copy(s).start())
    drain(0)
    drain(1)
    each(lambda s: stat_copy(s).wait_recv())
    gathered = every[...]
    average = jnp.sum(gathered[:, 0:1, :], axis=0) / population
    away = gathered[:, 3:4, :] - average[None]
    squares = jnp.sum(gathered[:, 1:2, :] + gathered[:, 2:3, :] * away * away, axis=0)
    gain = affine_ref[0:1, :] * (1.0 / jnp.sqrt(squares / population + 1e-05))
    bias = affine_ref[1:2, :]

    def finish(i, carry):
        value, full = rows_of(i)
        scaled = jnp.maximum((value - average) * gain + bias, 0.0)
        at = pl.ds(pl.multiple_of(i * BLOCK, BLOCK), BLOCK)
        out_ref[at, :] = jnp.where(full, scaled, 0.0).astype(jnp.bfloat16)
        return carry

    lax.fori_loop(0, blocks, finish, 0, unroll=4)
    each(lambda s: stat_copy(s).wait_send())


def layer(rim_blocks, outgoing, kernel_map, weights, affine, population):
    nx = lax.axis_size("tx")
    ny = lax.axis_size("ty")
    count = nx * ny
    _, blocks, block_half, channels = outgoing.shape
    rims = rim_blocks.shape[0] * rim_blocks.shape[1]
    offsets = weights.shape[0]
    smem = pl.BlockSpec(memory_space=pltpu.SMEM)
    vmem = pl.BlockSpec(memory_space=pltpu.VMEM)
    dma = pltpu.SemaphoreType.DMA
    return pl.pallas_call(
        functools.partial(layer_kernel, nx, ny, population),
        out_shape=jax.ShapeDtypeStruct((blocks * BLOCK, channels), jnp.bfloat16),
        in_specs=[smem, vmem, vmem, vmem, vmem],
        out_specs=vmem,
        scratch_shapes=[
            pltpu.VMEM((blocks * BLOCK, channels), jnp.float32),
            pltpu.VMEM((blocks, block_half, channels), jnp.bfloat16),
            pltpu.VMEM((blocks, block_half, channels), jnp.bfloat16),
            pltpu.VMEM((2, rims, block_half, channels), jnp.bfloat16),
            pltpu.VMEM((2, rims, block_half, channels), jnp.bfloat16),
            pltpu.VMEM((blocks, 128), jnp.int32),
            pltpu.SMEM((blocks, 128), jnp.int32),
            pltpu.VMEM(kernel_map.shape, jnp.int32),
            pltpu.VMEM((blocks + rims, channels // 2, 128), jnp.float32),
            pltpu.VMEM((2, channels, (offsets + 1) // 2 * channels), jnp.bfloat16),
            pltpu.VMEM((blocks // 4, channels, 256), jnp.float32),
            pltpu.VMEM((blocks // 2, 8, 128), jnp.float32),
            pltpu.VMEM((8, channels), jnp.float32),
            pltpu.VMEM((count, 8, channels), jnp.float32),
            dma((2, count)),
            dma((2, count)),
            dma((2, 4)),
            dma((2, 4)),
            dma((count,)),
            dma((count,)),
            dma(()),
        ],
        compiler_params=pltpu.CompilerParams(
            collective_id=1, has_side_effects=True, vmem_limit_bytes=48 * 1024 * 1024
        ),
    )(rim_blocks, outgoing, kernel_map, weights, affine)


def addresses(target, devices, pair_rows):
    src_count = target.shape[0]
    member = (target[:, None] == jnp.arange(devices, dtype=jnp.int32)[None, :]).astype(jnp.bfloat16)
    run_len = min(512, src_count)
    run_count = src_count // run_len
    member_runs = member.reshape(run_count, run_len, devices)
    lower_ones = (jnp.arange(run_len)[:, None] >= jnp.arange(run_len)[None, :]).astype(jnp.bfloat16)
    inside = jnp.einsum("ij,bjd->bid", lower_ones, member_runs, preferred_element_type=jnp.float32)
    run_totals = inside[:, -1, :]
    before = jnp.cumsum(run_totals, axis=0) - run_totals
    running = (inside + before[:, None, :]).reshape(src_count, devices)
    member_wide = member.astype(jnp.float32)
    placed = jnp.sum((running - 1.0) * member_wide, axis=1).astype(jnp.int32)
    return target * pair_rows + placed


def shards(voxels, owner_tile, rim_blocks, kernel_map, weights, norm_gain, shift_bias):
    devices = lax.axis_size(("tx", "ty"))
    channels = voxels.shape[1]
    tile_rows = kernel_map.shape[2]
    offsets = kernel_map.shape[1]
    pair_rows = tile_rows // devices
    address = addresses(owner_tile[:, 0], devices, pair_rows)
    outgoing = place(address, voxels, tile_rows)
    padded = jnp.pad(kernel_map[0], ((0, 32 - offsets), (0, 0)), constant_values=-1)
    population = float(voxels.shape[0] * devices)
    affine = jnp.stack((norm_gain, shift_bias))
    return layer(rim_blocks[0], outgoing, padded, weights, affine, population)


def solution(mesh):
    return jax.shard_map(
        shards,
        mesh=mesh,
        in_specs=(
            P(("tx", "ty"), None),
            P(("tx", "ty"), None),
            P(("tx", "ty"), None, None),
            P(("tx", "ty"), None, None),
            P(),
            P(),
            P(),
        ),
        out_specs=P(("tx", "ty"), None),
        check_vma=False,
    )
```

```python
import functools
import jax
import jax.numpy as jnp
from jax import lax
from jax.experimental import pallas as pl
from jax.experimental.pallas import tpu as pltpu
from jax.sharding import PartitionSpec as P

BLOCK = 64
MESH = pl.DeviceIdType.MESH


def place_kernel(address_ref, voxels_ref, out_ref, wide, slots):
    rows = voxels_ref.shape[0]
    total = slots.shape[0]
    chunk = 256

    def widen(i, carry):
        at = pl.ds(pl.multiple_of(i * chunk, chunk), chunk)
        wide[at, :] = voxels_ref[at, :].astype(jnp.float32)
        return carry

    def clear(i, carry):
        at = pl.ds(pl.multiple_of(i * chunk, chunk), chunk)
        slots[at, :] = jnp.full((chunk, slots.shape[1]), -1.0, jnp.float32)
        return carry

    def put(i, carry):
        base = pl.multiple_of(i * 16, 16)
        for u in range(16):
            slots[pl.ds(address_ref[base + u], 1), :] = wide[pl.ds(base + u, 1), :]
        return carry

    left = lax.broadcasted_iota(jnp.int32, (BLOCK // 2, slots.shape[1]), 1) < slots.shape[1] // 2

    def narrow(b, carry):
        block = slots[pl.ds(pl.multiple_of(b * BLOCK, BLOCK), BLOCK), :]
        upper, lower = block[: BLOCK // 2], block[BLOCK // 2 :]
        half = slots.shape[1] // 2
        out_ref[0, b] = jnp.where(left, upper, pltpu.roll(lower, half, 1)).astype(jnp.bfloat16)
        out_ref[1, b] = jnp.where(left, pltpu.roll(upper, half, 1), lower).astype(jnp.bfloat16)
        return carry

    lax.fori_loop(0, rows // chunk, widen, 0)
    lax.fori_loop(0, total // chunk, clear, 0)
    lax.fori_loop(0, rows // 16, put, 0)
    lax.fori_loop(0, total // BLOCK, narrow, 0, unroll=4)


def place(address, voxels, tile_rows):
    rows, channels = voxels.shape
    return pl.pallas_call(
        place_kernel,
        out_shape=jax.ShapeDtypeStruct(
            (2, tile_rows // BLOCK, BLOCK // 2, channels), jnp.bfloat16
        ),
        in_specs=[
            pl.BlockSpec(memory_space=pltpu.SMEM),
            pl.BlockSpec(memory_space=pltpu.VMEM),
        ],
        out_specs=pl.BlockSpec(memory_space=pltpu.VMEM),
        scratch_shapes=[
            pltpu.VMEM((rows, channels), jnp.float32),
            pltpu.VMEM((tile_rows, channels), jnp.float32),
        ],
        compiler_params=pltpu.CompilerParams(vmem_limit_bytes=32 * 1024 * 1024),
    )(address, voxels)


def partner(nx, ny, s):
    tx = lax.rem(lax.axis_index("tx") + lax.rem(s, nx), nx)
    ty = lax.rem(lax.axis_index("ty") + s // nx, ny)
    return tx, ty


def layer_kernel(
    nx, ny, population, rim_ref, outgoing_ref, map_ref, weights_ref, affine_ref, out_ref, resp_ref,
    arrival0, arrival1, staged, rims, found_v, found_s, spots, table, turned, partial, filled, mine, every,
    send, recv, rim_send, rim_recv, stat_send, stat_recv, local_sem
):
    tx = lax.axis_index("tx")
    ty = lax.axis_index("ty")
    me = tx * ny + ty
    count = nx * ny
    arrival = (arrival0, arrival1)
    blocks = arrival0.shape[0]
    per = blocks // count
    rim = rims.shape[1] // 4
    offsets = weights_ref.shape[0]
    channels = weights_ref.shape[1]
    half = channels // 2
    middle = offsets // 2
    order = [k for k in range(offsets) if k != middle] + [middle]

    barrier = pltpu.get_barrier_semaphore()

    def call(s, carry):
        pl.semaphore_signal(barrier, inc=1, device_id=partner(nx, ny, s), device_id_type=MESH)
        return carry

    lax.fori_loop(1, count, call, 0)
    pl.semaphore_wait(barrier, count - 1)

    def copy(h, s):
        px, py = partner(nx, ny, s)
        return pltpu.make_async_remote_copy(
            src_ref=outgoing_ref.at[h, pl.ds((px * ny + py) * per, per)],
            dst_ref=arrival[h].at[pl.ds(me * per, per)],
            send_sem=send.at[h, s],
            recv_sem=recv.at[h, s],
            device_id=(px, py),
            device_id_type=MESH,
        )

    def each(act):
        def step(s, carry):
            act(s)
            return carry

        lax.fori_loop(1, count, step, 0)

    ways = (
        (0, (tx + 1, ty), tx < nx - 1, tx > 0),
        (1, (tx - 1, ty), tx > 0, tx < nx - 1),
        (2, (tx, ty + 1), ty < ny - 1, ty > 0),
        (3, (tx, ty - 1), ty > 0, ty < ny - 1),
    )

    def rim_copy(h, number, to):
        return pltpu.make_async_remote_copy(
            src_ref=staged.at[h, pl.ds(number * rim, rim)],
            dst_ref=rims.at[h, pl.ds(number * rim, rim)],
            send_sem=rim_send.at[h, number],
            recv_sem=rim_recv.at[h, number],
            device_id=to,
            device_id_type=MESH,
        )

    def send_rims(h):
        def stage(i, carry):
            for number in range(4):
                staged[h, number * rim + i] = arrival[h][rim_ref[number, i]]
            return carry

        lax.fori_loop(0, rim, stage, 0)
        for number, to, sends, takes in ways:

            @pl.when(sends)
            def _():
                rim_copy(h, number, to).start()

            @pl.when(jnp.logical_not(takes))
            def _():
                rims[h, pl.ds(number * rim, rim)] = jnp.zeros((rim,) + rims.shape[2:], jnp.bfloat16)

    def take_rims(h):
        for number, to, sends, takes in ways:

            @pl.when(takes)
            def _():
                rim_copy(h, number, to).wait_recv()

    def drain(h):
        each(lambda s: copy(h, s).wait_send())
        for number, to, sends, takes in ways:

            @pl.when(sends)
            def _():
                rim_copy(h, number, to).wait_send()

    each(lambda s: copy(0, s).start())
    for h in range(2):
        for q in range(per):
            arrival[h][me * per + q] = outgoing_ref[h, me * per + q]

    found_v[...] = jnp.zeros_like(found_v)

    second = jnp.where(
        lax.broadcasted_iota(jnp.int32, (map_ref.shape[0], 128), 1) < BLOCK, 0, BLOCK
    )

    def prepare(c, carry):
        at = pl.ds(pl.multiple_of(c * 128, 128), 128)
        entries = map_ref[:, at]
        spots[:, at] = jnp.bitwise_and(entries, BLOCK - 1) + second
        columns = entries.T
        for i in range(2):
            rows = columns[i * BLOCK : (i + 1) * BLOCK]
            source = jnp.maximum(jnp.max(rows, axis=0, keepdims=True), 0) // BLOCK
            found_v[pl.ds(2 * c + i, 1), 0 : map_ref.shape[0]] = source
        return carry

    lax.fori_loop(0, blocks // 2, prepare, 0)
    inward = pltpu.make_async_copy(found_v, found_s, local_sem)
    inward.start()

    row_at = lax.broadcasted_iota(jnp.int32, (channels, channels), 0)
    lane_at = lax.broadcasted_iota(jnp.int32, (channels, channels), 1)
    unit = jnp.where(row_at == lane_at, 1.0, 0.0).astype(jnp.bfloat16)
    top_at = lax.broadcasted_iota(jnp.int32, (half, 2 * channels), 0)
    wide_at = lax.broadcasted_iota(jnp.int32, (half, 2 * channels), 1)
    halves = (wide_at == top_at) | (wide_at == top_at + channels + half)
    halves = jnp.where(halves, 1.0, 0.0).astype(jnp.bfloat16)
    left = lane_at[:half] < BLOCK

    def flip(value, by):
        return lax.dot_general(
            by, value, (((1,), (1,)), ((), ())), preferred_element_type=jnp.float32
        )

    nothing16 = jnp.zeros((half, channels), jnp.bfloat16)
    for h in range(2):
        for p in range((offsets + 1) // 2):
            one = weights_ref[order[2 * p]][h * half : (h + 1) * half]
            two = nothing16
            if 2 * p + 1 < offsets:
                two = weights_ref[order[2 * p + 1]][h * half : (h + 1) * half]
            turned[h, :, p * channels : (p + 1) * channels] = flip(
                jnp.concatenate((one, two), axis=0), unit
            ).astype(jnp.bfloat16)
    inward.wait()

    quiet = jnp.zeros((BLOCK // 2, channels), jnp.bfloat16)

    def block_table(block):
        first = jnp.concatenate((block, quiet, block, quiet), axis=0)
        second = jnp.concatenate((quiet, block, quiet, block), axis=0)
        return flip(jnp.concatenate((first, second), axis=1), halves)

    def fill_tile(h):
        def step(c, carry):
            one = block_table(arrival[h][2 * c])
            two = block_table(arrival[h][2 * c + 1])
            table[2 * c] = jnp.maximum(one, 0.0)
            table[2 * c + 1] = jnp.maximum(two, 0.0)
            if h == 1:
                filled[c] = jnp.where(left[:8], one[:8], two[:8])
            return carry

        lax.fori_loop(0, blocks // 2, step, 0, unroll=4)

    def fill_rims(h):
        def step(i, carry):
            table[blocks + i] = jnp.maximum(block_table(rims[h, i]), 0.0)
            return carry

        lax.fori_loop(0, 4 * rim, step, 0, unroll=4)

    marker = -1e30

    def convolve(h, first, last):
        def window(w, carry):
            def pick(k, c):
                b = 2 * (2 * w + c)
                if k == middle:
                    return jnp.where(left, table[b], table[b + 1]).astype(jnp.bfloat16)
                at = pl.ds(pl.multiple_of((2 * w + c) * 128, 128), 128)
                entry = map_ref[k : k + 1, at]
                spot = jnp.broadcast_to(spots[k : k + 1, at], (half, 128))
                source = jnp.where(left, table[found_s[b, k]], table[found_s[b + 1, k]])
                taken = jnp.take_along_axis(source, spot, axis=1)
                return jnp.where(entry >= 0, taken, 0.0).astype(jnp.bfloat16)

            result = None
            for p in range((offsets + 3) // 4):
                parts = [
                    jnp.concatenate((pick(k, 0), pick(k, 1)), axis=1)
                    for k in order[4 * p : 4 * p + 4]
                ]
                while len(parts) % 2:
                    parts.append(jnp.zeros((half, 256), jnp.bfloat16))
                depth = len(parts) * half
                term = jnp.dot(
                    turned[h, :, p * 4 * half : p * 4 * half + depth],
                    jnp.concatenate(parts, axis=0),
                    preferred_element_type=jnp.float32,
                )
                result = term if result is None else result + term
            if h == 0:
                partial[w] = result
            else:
                result = result + partial[w]
                for c in range(2):
                    here = filled[2 * w + c][0:1] >= 0.0
                    rows = jnp.where(here, result[:, c * 128 : (c + 1) * 128], marker).T
                    resp_ref[pl.ds(pl.multiple_of((2 * w + c) * 128, 128), 128), :] = rows
            return carry

        lax.fori_loop(first, last, window, 0, unroll=2)

    each(lambda s: copy(0, s).wait_recv())
    send_rims(0)
    fill_tile(0)
    take_rims(0)
    each(lambda s: copy(1, s).start())
    fill_rims(0)
    windows = blocks // 4
    split = windows * 7 // 8
    convolve(0, 0, split)
    each(lambda s: copy(1, s).wait_recv())
    send_rims(1)
    convolve(0, split, windows)
    fill_tile(1)
    take_rims(1)
    fill_rims(1)
    convolve(1, 0, windows)

    def rows_of(i):
        value = resp_ref[pl.ds(pl.multiple_of(i * BLOCK, BLOCK), BLOCK), :]
        return value, value > marker * 0.5

    def fold(value):
        return jnp.sum(value.reshape(BLOCK // 8, 8, channels), axis=0)

    def add(i, carry):
        value, full = rows_of(i)
        return (
            carry[0] + fold(jnp.where(full, value, 0.0)),
            carry[1] + fold(jnp.where(full, 1.0, 0.0)),
        )

    nothing = jnp.zeros((8, channels), jnp.float32)
    total, number = lax.fori_loop(0, blocks, add, (nothing, nothing), unroll=4)
    total = jnp.sum(total, axis=0, keepdims=True)
    number = jnp.sum(number, axis=0, keepdims=True)
    mean = total / jnp.maximum(number, 1.0)

    def spread_of(i, squares):
        value, full = rows_of(i)
        off = jnp.where(full, value - mean, 0.0)
        return squares + fold(off * off)

    squares = lax.fori_loop(0, blocks, spread_of, nothing, unroll=4)
    squares = jnp.sum(squares, axis=0, keepdims=True)
    row = lax.broadcasted_iota(jnp.int32, (8, channels), 0)
    stats = jnp.where(
        row == 0, total, jnp.where(row == 1, squares, jnp.where(row == 2, number, mean))
    )
    mine[...] = stats
    every[0] = stats

    def stat_copy(s):
        return pltpu.make_async_remote_copy(
            src_ref=mine,
            dst_ref=every.at[s],
            send_sem=stat_send.at[s],
            recv_sem=stat_recv.at[s],
            device_id=partner(nx, ny, s),
            device_id_type=MESH,
        )

    each(lambda s: stat_copy(s).start())
    drain(0)
    drain(1)
    each(lambda s: stat_copy(s).wait_recv())
    gathered = every[...]
    average = jnp.sum(gathered[:, 0:1, :], axis=0) / population
    away = gathered[:, 3:4, :] - average[None]
    squares = jnp.sum(gathered[:, 1:2, :] + gathered[:, 2:3, :] * away * away, axis=0)
    gain = affine_ref[0:1, :] * (1.0 / jnp.sqrt(squares / population + 1e-05))
    bias = affine_ref[1:2, :]

    def finish(i, carry):
        value, full = rows_of(i)
        scaled = jnp.maximum((value - average) * gain + bias, 0.0)
        at = pl.ds(pl.multiple_of(i * BLOCK, BLOCK), BLOCK)
        out_ref[at, :] = jnp.where(full, scaled, 0.0).astype(jnp.bfloat16)
        return carry

    lax.fori_loop(0, blocks, finish, 0, unroll=4)
    each(lambda s: stat_copy(s).wait_send())


def layer(rim_blocks, outgoing, kernel_map, weights, affine, population):
    nx = lax.axis_size("tx")
    ny = lax.axis_size("ty")
    count = nx * ny
    _, blocks, block_half, channels = outgoing.shape
    rims = rim_blocks.shape[0] * rim_blocks.shape[1]
    offsets = weights.shape[0]
    smem = pl.BlockSpec(memory_space=pltpu.SMEM)
    vmem = pl.BlockSpec(memory_space=pltpu.VMEM)
    dma = pltpu.SemaphoreType.DMA
    return pl.pallas_call(
        functools.partial(layer_kernel, nx, ny, population),
        out_shape=jax.ShapeDtypeStruct((blocks * BLOCK, channels), jnp.bfloat16),
        in_specs=[smem, vmem, vmem, vmem, vmem],
        out_specs=vmem,
        scratch_shapes=[
            pltpu.VMEM((blocks * BLOCK, channels), jnp.float32),
            pltpu.VMEM((blocks, block_half, channels), jnp.bfloat16),
            pltpu.VMEM((blocks, block_half, channels), jnp.bfloat16),
            pltpu.VMEM((2, rims, block_half, channels), jnp.bfloat16),
            pltpu.VMEM((2, rims, block_half, channels), jnp.bfloat16),
            pltpu.VMEM((blocks, 128), jnp.int32),
            pltpu.SMEM((blocks, 128), jnp.int32),
            pltpu.VMEM(kernel_map.shape, jnp.int32),
            pltpu.VMEM((blocks + rims, channels // 2, 128), jnp.float32),
            pltpu.VMEM((2, channels, (offsets + 1) // 2 * channels), jnp.bfloat16),
            pltpu.VMEM((blocks // 4, channels, 256), jnp.float32),
            pltpu.VMEM((blocks // 2, 8, 128), jnp.float32),
            pltpu.VMEM((8, channels), jnp.float32),
            pltpu.VMEM((count, 8, channels), jnp.float32),
            dma((2, count)),
            dma((2, count)),
            dma((2, 4)),
            dma((2, 4)),
            dma((count,)),
            dma((count,)),
            dma(()),
        ],
        compiler_params=pltpu.CompilerParams(
            collective_id=1, has_side_effects=True, vmem_limit_bytes=48 * 1024 * 1024
        ),
    )(rim_blocks, outgoing, kernel_map, weights, affine)


def addresses(target, devices, pair_rows):
    src_count = target.shape[0]
    member = (target[:, None] == jnp.arange(devices, dtype=jnp.int32)[None, :]).astype(jnp.bfloat16)
    run_len = min(512, src_count)
    run_count = src_count // run_len
    member_runs = member.reshape(run_count, run_len, devices)
    lower_ones = (jnp.arange(run_len)[:, None] >= jnp.arange(run_len)[None, :]).astype(jnp.bfloat16)
    inside = jnp.einsum("ij,bjd->bid", lower_ones, member_runs, preferred_element_type=jnp.float32)
    run_totals = inside[:, -1, :]
    before = jnp.cumsum(run_totals, axis=0) - run_totals
    running = (inside + before[:, None, :]).reshape(src_count, devices)
    member_wide = member.astype(jnp.float32)
    placed = jnp.sum((running - 1.0) * member_wide, axis=1).astype(jnp.int32)
    return target * pair_rows + placed


def shards(voxels, owner_tile, rim_blocks, kernel_map, weights, norm_gain, shift_bias):
    devices = lax.axis_size(("tx", "ty"))
    channels = voxels.shape[1]
    tile_rows = kernel_map.shape[2]
    offsets = kernel_map.shape[1]
    pair_rows = tile_rows // devices
    address = addresses(owner_tile[:, 0], devices, pair_rows)
    outgoing = place(address, voxels, tile_rows)
    padded = jnp.pad(kernel_map[0], ((0, 32 - offsets), (0, 0)), constant_values=-1)
    population = float(voxels.shape[0] * devices)
    affine = jnp.stack((norm_gain, shift_bias))
    return layer(rim_blocks[0], outgoing, padded, weights, affine, population)


def solution(mesh):
    return jax.shard_map(
        shards,
        mesh=mesh,
        in_specs=(
            P(("tx", "ty"), None),
            P(("tx", "ty"), None),
            P(("tx", "ty"), None, None),
            P(("tx", "ty"), None, None),
            P(),
            P(),
            P(),
        ),
        out_specs=P(("tx", "ty"), None),
        check_vma=False,
    )
```
